32 devices in a mesh: sub: 8 (over z, y), grp: 4 (over x, core).
Axes of the slice: x: 2, y: 2, z: 4, core: 2. Of those that a mesh axis runs over, the one named last changes fastest.
Arguments:
- residual: float32 [16, 8, 4, 512], P(None, 'sub', 'grp'), may hold values from -6 to 6
- bounds: float32 [2], replicated, may hold values from 0.2 to 14, as said below
- local_inverse: bfloat16 [8, 4, 1024, 1024], P('sub', 'grp'), may hold values from -1 to 2
- corner_basis: bfloat16 [8, 4, 24, 1024], P('sub', 'grp'), may hold values from -1 to 1
- corner_map: int32 [8, 4, 24], P('sub', 'grp'), may hold values from 0 to 31
- coarse_inverse: float32 [32, 32], P(('sub', 'grp')), may hold values from -1 to 2, as said below
Outputs:
- basis: float32 [5, 16, 8, 4, 512], P(None, None, 'sub', 'grp')
- gram: float32 [80, 80], replicated
The draws below stay inside these ranges and needn't reach their ends.
Inputs may be any that keep to these rules, and one draw needn't show every extreme that they name: bounds[0] lies in 0.2 to 0.4 and bounds[1] in 10 to 14. `coarse_inverse`: symmetric.
All inputs are finite; a program needn't handle non-finite values.
Results may differ from the reference program's by a relative error of at most 0.0022.
Values may be sent and summed in bfloat16 or wider, within the bound.
A program may use at most 64 MiB of HBM per device.

```python
import jax
import jax.numpy as jnp
from jax import lax

FACE = 256
RHS = 16
S_STEP = 2
CORNERS = 24
CO_DEV = 1
NSUBS = 8
NGRPS = 4
NCO = 32
GRAM = 80


def draw_bounds(key, part):
    first, second = jax.random.split(jax.random.fold_in(key, 11))
    lower = jax.random.uniform(first, (), jnp.float32, 0.2, 0.4)
    upper = jax.random.uniform(second, (), jnp.float32, 10.0, 14.0)
    return jnp.stack([lower, upper])


def draw_local_inverse(key, part):
    width = 4 * FACE
    first, second = jax.random.split(jax.random.fold_in(key, 23))
    diagonal_part = jax.random.uniform(first, (NSUBS, NGRPS, width), jnp.float32, 0.5, 1.0)
    noise_part = jax.random.normal(second, (NSUBS, NGRPS, width, width), jnp.float32) * (0.35 / jnp.sqrt(1.0 * width))
    noise_part = jnp.clip(noise_part, -0.5, 0.5)
    whole = noise_part + diagonal_part[..., None] * jnp.eye(width, dtype=jnp.float32)
    return whole.astype(jnp.bfloat16)


def draw_corner_basis(key, part):
    width = 4 * FACE
    spread = jnp.sqrt(4.0 * CO_DEV / (1.0 * CORNERS * width))
    values = jax.random.normal(jax.random.fold_in(key, 53), (NSUBS, NGRPS, CORNERS, width), jnp.float32)
    values = jnp.clip(values, -4.0, 4.0) * spread
    return values.astype(jnp.bfloat16)


def draw_coarse_inverse(key, part):
    first, second = jax.random.split(jax.random.fold_in(key, 37))
    diagonal_part = jnp.exp(jax.random.uniform(first, (NCO,), jnp.float32, jnp.log(0.3), 0.0))
    noise_part = jax.random.normal(second, (NCO, NCO), jnp.float32) * (0.4 / jnp.sqrt(1.0 * NCO))
    noise_part = jnp.clip(0.5 * (noise_part + noise_part.T), -0.5, 0.5)
    return noise_part + diagonal_part[:, None] * jnp.eye(NCO, dtype=jnp.float32)


def touch_ends(array, own_key, smallest, high):
    longest = array.shape.index(max(array.shape))
    spots = []
    for shift in (0, 1):
        where = [jax.random.randint(jax.random.fold_in(own_key, axis), (), 0, length) for axis, length in enumerate(array.shape)]
        where[longest] = (where[longest] + shift) % array.shape[longest]
        spots.append(tuple(where))
    return array.at[spots[0]].set(smallest).at[spots[1]].set(high)


def levels(stream_key, extent, pieces, smallest, top_value):
    loudness, own = 1.0, jax.random.fold_in(stream_key, 6)
    for position, parts in pieces:
        steps = jnp.exp(jax.random.uniform(jax.random.fold_in(own, position), (parts,), jnp.float32, smallest / len(pieces), top_value / len(pieces)))
        loudness = loudness * jnp.repeat(steps, extent[position] // parts).reshape([-1 if axis == position else 1 for axis in range(len(extent))])
    return loudness


def scatter_about(rng, shape, scale, reach, shards=(), held_as=jnp.bfloat16):
    factor_of = levels(rng, shape, shards, -0.22, 0.18) if shards else 1.0
    drawn = jax.random.normal(rng, shape, jnp.float32) * scale * factor_of
    return jnp.minimum(jnp.maximum(drawn, -reach), reach).astype(held_as)


def setup_inputs(seed: int = 0) -> dict:
    arg_keys = jax.random.split(jax.random.key(seed), 7)
    residual = scatter_about(arg_keys[0], (RHS, NSUBS, NGRPS, 2 * FACE), 1.0, 6.0, ((1, 8), (2, 4)), jnp.float32)
    bounds = draw_bounds(jax.random.fold_in(arg_keys[6], 71), 0)
    local_inverse = draw_local_inverse(jax.random.fold_in(arg_keys[6], 71), 0)
    corner_basis = draw_corner_basis(jax.random.fold_in(arg_keys[6], 71), 0)
    corner_map = touch_ends(jax.random.randint(arg_keys[4], (NSUBS, NGRPS, CORNERS), 0, NCO), jax.random.fold_in(arg_keys[4], 1), 0, NCO - 1).astype(jnp.int32)
    coarse_inverse = draw_coarse_inverse(jax.random.fold_in(arg_keys[6], 71), 0)
    return dict(residual=residual, bounds=bounds, local_inverse=local_inverse, corner_basis=corner_basis, corner_map=corner_map, coarse_inverse=coarse_inverse)


def apply_operator(block, local_inverse, corners_wide, corner_table, coarse_inverse):
    width = 4 * FACE
    packed = block.astype(jnp.bfloat16)
    up_sub = packed[..., :FACE]
    up_grp = packed[..., FACE:]
    low_sub = jnp.roll(up_sub, 1, axis=1)
    low_grp = jnp.roll(up_grp, 1, axis=2)
    load_rows = jnp.concatenate([up_sub, -low_sub, up_grp, -low_grp], axis=-1)
    per_device = jnp.transpose(load_rows, (1, 2, 0, 3)).reshape(NSUBS * NGRPS, RHS, width)
    inverses = local_inverse.reshape(NSUBS * NGRPS, width, width)
    local_part = lax.map(lambda pair: jnp.dot(pair[0], pair[1], preferred_element_type=jnp.float32), (per_device, inverses))
    weights = jnp.einsum('drk,dck->drc', per_device.astype(jnp.float32), corners_wide, precision=lax.Precision.HIGHEST)
    coarse_load = jnp.einsum('drc,dcn->rn', weights, corner_table, precision=lax.Precision.HIGHEST)
    coarse_value = jnp.dot(coarse_load, coarse_inverse, precision=lax.Precision.HIGHEST)
    picked = jnp.einsum('rn,dcn->drc', coarse_value, corner_table, precision=lax.Precision.HIGHEST)
    displaced = local_part + jnp.einsum('drc,dck->drk', picked, corners_wide, precision=lax.Precision.HIGHEST)
    displaced = displaced.reshape(NSUBS, NGRPS, RHS, width)
    jump_sub = displaced[..., :FACE] - jnp.roll(displaced[..., FACE:2 * FACE], -1, axis=0)
    jump_grp = displaced[..., 2 * FACE:3 * FACE] - jnp.roll(displaced[..., 3 * FACE:], -1, axis=1)
    return jnp.transpose(jnp.concatenate([jump_sub, jump_grp], axis=-1), (2, 0, 1, 3))


def reference(residual, bounds, local_inverse, corner_basis, corner_map, coarse_inverse):
    centre = (bounds[0] + bounds[1]) / 2.0
    radius = (bounds[1] - bounds[0]) / 2.0
    corners_wide = corner_basis.reshape(NSUBS * NGRPS, CORNERS, 4 * FACE).astype(jnp.float32)
    corner_ids = corner_map.reshape(NSUBS * NGRPS, CORNERS)
    corner_table = (corner_ids[:, :, None] == jnp.arange(NCO, dtype=jnp.int32)[None, None, :]).astype(jnp.float32)
    previous = residual
    image = apply_operator(previous, local_inverse, corners_wide, corner_table, coarse_inverse)
    current = (image - centre * previous) / radius
    blocks = [previous, current]
    for level in range(1, 2 * S_STEP):
        image = apply_operator(current, local_inverse, corners_wide, corner_table, coarse_inverse)
        following = 2.0 * (image - centre * current) / radius - previous
        blocks.append(following)
        previous, current = current, following
    basis = jnp.stack(blocks)
    merged = basis.reshape(GRAM, -1)
    gram = jnp.dot(merged, merged.T, precision=lax.Precision.HIGHEST) / (2.0 * FACE * NSUBS)
    return basis, gram
```

```python
import functools

import jax
import jax.numpy as jnp
from jax import lax
from jax.experimental import pallas as pl
from jax.experimental.pallas import tpu as pltpu
from jax.sharding import PartitionSpec as P

S_STEP = 2
BLOCKS = 2 * S_STEP + 1
LEVELS = 2 * S_STEP
MESH = pl.DeviceIdType.MESH
HIGHEST = lax.Precision.HIGHEST


def exact(a, b):
    return jnp.dot(a, b, precision=HIGHEST, preferred_element_type=jnp.float32)


def across_rows(a, b, precision=None):
    return lax.dot_general(
        a, b, (((1,), (1,)), ((), ())), precision=precision, preferred_element_type=jnp.float32
    )


def dot(a, b):
    return jnp.dot(a, b, preferred_element_type=jnp.float32)


def kernel(
    nsub, ngrp, inner,
    bounds_ref, res_ref, inv_hbm, corner_ref, map_ref, coarse_ref,
    basis_ref, gram_ref,
    inv, up_out, up_in, low_out, low_in, term_out, term_in, rows_c, near, far, load_w, vec, lift,
    inv_sem, up_send, up_recv, low_send, low_recv, term_send, term_recv,
    rows_send, rows_recv, near_send, near_recv, far_send, far_recv,
):
    right, half = up_out.shape[2], vec.shape[1]
    face = half // 2
    order = BLOCKS * right
    nco = coarse_ref.shape[1]
    planes = nsub // inner
    members = inner * ngrp
    sub = lax.axis_index("sub")
    grp = lax.axis_index("grp")
    plane = lax.div(sub, inner)
    within = lax.rem(sub, inner)
    member = within * ngrp + grp
    next_sub = (lax.rem(sub + 1, nsub), grp)
    prev_sub = (lax.rem(sub + nsub - 1, nsub), grp)
    next_grp = (sub, lax.rem(grp + 1, ngrp))
    prev_grp = (sub, lax.rem(grp + ngrp - 1, ngrp))

    def near_peer(offset):
        other = lax.rem(member + offset, members)
        return (plane * inner + lax.div(other, ngrp), lax.rem(other, ngrp))

    def far_peer(offset):
        return (lax.rem(plane + offset, planes) * inner + within, grp)

    near_peers = [near_peer(o) for o in range(1, members)]
    far_peers = [far_peer(o) for o in range(1, planes)]

    barrier = pltpu.get_barrier_semaphore()
    greeted = near_peers + far_peers + [next_sub, prev_sub]
    for peer in greeted:
        pl.semaphore_signal(barrier, inc=1, device_id=peer, device_id_type=MESH)
    load_inv = pltpu.make_async_copy(inv_hbm.at[0, 0], inv, inv_sem)
    load_inv.start()

    def send(src, dst, send_sem, recv_sem, peer):
        copy = pltpu.make_async_remote_copy(
            src_ref=src, dst_ref=dst, send_sem=send_sem, recv_sem=recv_sem,
            device_id=peer, device_id_type=MESH,
        )
        copy.start()
        return copy

    centre = (bounds_ref[0] + bounds_ref[1]) / 2.0
    radius = (bounds_ref[1] - bounds_ref[0]) / 2.0
    scale = 1.0 / jnp.full((right, half), radius, jnp.float32)
    x = res_ref[:, 0, 0, :]
    vec[...] = jnp.zeros_like(vec)
    load_w[...] = jnp.zeros_like(load_w)
    lift[...] = jnp.zeros_like(lift)
    corners = corner_ref[0, 0]
    ids = map_ref[0]
    table = (lax.broadcasted_iota(jnp.int32, (nco, ids.shape[1]), 0) == ids).astype(jnp.bfloat16)
    terms = dot(table, corners)
    term_out[0] = terms[:, face : 2 * face]
    term_out[1] = terms[:, 3 * face :]
    rows_c[plane, member] = coarse_ref[...]

    def all_but_one(buf, count):
        return buf.at[pl.ds(0, count - 1)]

    def drain(ref, send_sem, recv_sem, peer):
        return pltpu.make_async_remote_copy(
            src_ref=ref, dst_ref=ref, send_sem=send_sem, recv_sem=recv_sem,
            device_id=peer, device_id_type=MESH,
        )

    pending = []

    def start_near(level, message):
        near[level, member] = message
        for peer in near_peers:
            own = near.at[level, member]
            send(own, own, near_send.at[level], near_recv.at[level], peer)

    def pass_far(level):
        landed = drain(all_but_one(near.at[level], members), near_send.at[level], near_recv.at[level], near_peers[0])
        landed.wait_recv()
        pending.append(landed)
        total = near[level, 0]
        for i in range(1, members):
            total = total + near[level, i]
        far[level, plane] = total
        for peer in far_peers:
            own = far.at[level, plane]
            send(own, own, far_send.at[level], far_recv.at[level], peer)

    def finish(level):
        landed = drain(all_but_one(far.at[level], planes), far_send.at[level], far_recv.at[level], far_peers[0])
        landed.wait_recv()
        pending.append(landed)
        total = far[level, 0]
        for i in range(1, planes):
            total = total + far[level, i]
        return total

    pl.semaphore_wait(barrier, len(greeted))

    gram_rows = []
    previous = None
    for level in range(LEVELS):
        packed = x.astype(jnp.bfloat16)
        x_sub, x_grp = packed[:, :face], packed[:, face:]
        up_out[level, 0] = x_sub
        up_out[level, 1] = x_grp
        ups = [
            send(up_out.at[level, d], up_in.at[level, d], up_send.at[level, d], up_recv.at[level, d], peer)
            for d, peer in enumerate((next_sub, next_grp))
        ]
        pending += ups
        if level == 0:
            term_copies = [
                send(term_out.at[d], term_in.at[d], term_send.at[d], term_recv.at[d], peer)
                for d, peer in enumerate((prev_sub, prev_grp))
            ]
            pending += term_copies
            for peer in near_peers:
                own = rows_c.at[plane, member]
                send(own, own, rows_send.at[0], rows_recv.at[0], peer)
        basis_ref[level, :, 0, 0, :] = x
        vec[pl.ds(level * right, right), :] = x

        def message():
            return (
                across_rows(packed, load_w[0])
                + across_rows(packed, load_w[1])
                + across_rows(x, vec[...], HIGHEST)
            )

        if level > 0:
            start_near(level, message())
        else:
            load_inv.wait()
        own = dot(x_sub, inv[:face, :]) + dot(x_grp, inv[2 * face : 3 * face, :])
        for copy in ups:
            copy.wait_recv()
        low_sub = up_in[level, 0]
        low_grp = up_in[level, 1]

        def displaced(first):
            columns = slice(first, first + face)
            return (
                own[:, columns]
                - dot(low_sub, inv[face : 2 * face, columns])
                - dot(low_grp, inv[3 * face :, columns])
            )

        low_out[level, 0] = displaced(face)
        low_out[level, 1] = displaced(3 * face)
        lows = [
            send(low_out.at[level, d], low_in.at[level, d], low_send.at[level, d], low_recv.at[level, d], peer)
            for d, peer in enumerate((prev_sub, prev_grp))
        ]
        pending += lows
        if level == 0:
            for copy in term_copies:
                copy.wait_recv()
            rows = slice(order, order + nco)
            weight = jnp.concatenate(
                [terms[:, :face] - term_in[0], terms[:, 2 * face : 3 * face] - term_in[1]], axis=1
            )
            rough = weight.astype(jnp.bfloat16)
            load_w[0, rows, :] = rough
            load_w[1, rows, :] = (weight - rough.astype(jnp.float32)).astype(jnp.bfloat16)
            start_near(level, message())
            landed = drain(all_but_one(rows_c.at[plane], members), rows_send.at[0], rows_recv.at[0], near_peers[0])
            landed.wait_recv()
            pending.append(landed)
            for peer in far_peers:
                mine = rows_c.at[plane]
                send(mine, mine, rows_send.at[1], rows_recv.at[1], peer)
        up = jnp.concatenate([displaced(0), displaced(2 * face)], axis=1)
        pass_far(level)
        if level == 0:
            landed = drain(all_but_one(rows_c, planes), rows_send.at[1], rows_recv.at[1], far_peers[0])
            landed.wait_recv()
            pending.append(landed)
            lift[rows, :] = exact(rows_c[...].reshape(nco, nco), weight)
        total = finish(level)
        gram_rows.append(total)
        image = up + exact(total, lift[...])
        for copy in lows:
            copy.wait_recv()
        image = image - jnp.concatenate([low_in[level, 0], low_in[level, 1]], axis=1)
        if level == 0:
            following = (image - centre * x) * scale
        else:
            following = 2.0 * (image - centre * x) * scale - previous
        previous, x = x, following

    basis_ref[LEVELS, :, 0, 0, :] = x
    vec[pl.ds(LEVELS * right, right), :] = x
    start_near(LEVELS, across_rows(x, vec[...], HIGHEST))
    pass_far(LEVELS)
    gram_rows.append(finish(LEVELS))
    full = jnp.concatenate(gram_rows, axis=0)[:, :order]
    row = lax.broadcasted_iota(jnp.int32, (order, order), 0)
    column = lax.broadcasted_iota(jnp.int32, (order, order), 1)
    below = jnp.where(lax.div(column, right) < lax.div(row, right), full, 0.0)
    same = jnp.where(lax.div(column, right) == lax.div(row, right), full, 0.0)
    gram_ref[...] = (below + same + below.T) * (1.0 / (half * nsub))
    for copy in pending:
        copy.wait_send()


def body(nsub, ngrp, residual, bounds, local_inverse, corner_basis, corner_map, coarse_inverse):
    right, half = residual.shape[0], residual.shape[3]
    face = half // 2
    width = 4 * face
    rows, nco = coarse_inverse.shape
    order = BLOCKS * right
    inner = 1
    while nsub % (2 * inner) == 0 and 2 * inner * ngrp <= nsub // inner:
        inner *= 2
    planes, members = nsub // inner, inner * ngrp
    wide = -(-(order + nco) // 128) * 128
    vmem = pl.BlockSpec(memory_space=pltpu.VMEM)
    dma = pltpu.SemaphoreType.DMA
    f32, bf16 = jnp.float32, jnp.bfloat16
    return pl.pallas_call(
        functools.partial(kernel, nsub, ngrp, inner),
        out_shape=(
            jax.ShapeDtypeStruct((BLOCKS, right, 1, 1, half), f32),
            jax.ShapeDtypeStruct((order, order), f32),
        ),
        in_specs=[
            pl.BlockSpec(memory_space=pltpu.SMEM),
            vmem,
            pl.BlockSpec(memory_space=pl.ANY),
            vmem,
            vmem,
            vmem,
        ],
        out_specs=(vmem, vmem),
        scratch_shapes=[
            pltpu.VMEM((width, width), bf16),
            pltpu.VMEM((LEVELS, 2, right, face), bf16),
            pltpu.VMEM((LEVELS, 2, right, face), bf16),
            pltpu.VMEM((LEVELS, 2, right, face), f32),
            pltpu.VMEM((LEVELS, 2, right, face), f32),
            pltpu.VMEM((2, nco, face), f32),
            pltpu.VMEM((2, nco, face), f32),
            pltpu.VMEM((planes, members, rows, nco), f32),
            pltpu.VMEM((BLOCKS, members, right, wide), f32),
            pltpu.VMEM((BLOCKS, planes, right, wide), f32),
            pltpu.VMEM((2, wide, half), bf16),
            pltpu.VMEM((wide, half), f32),
            pltpu.VMEM((wide, half), f32),
            dma,
            dma((LEVELS, 2)),
            dma((LEVELS, 2)),
            dma((LEVELS, 2)),
            dma((LEVELS, 2)),
            dma((2,)),
            dma((2,)),
            dma((2,)),
            dma((2,)),
            dma((BLOCKS,)),
            dma((BLOCKS,)),
            dma((BLOCKS,)),
            dma((BLOCKS,)),
        ],
        compiler_params=pltpu.CompilerParams(
            collective_id=0, has_side_effects=True, vmem_limit_bytes=48 * 1024 * 1024
        ),
    )(bounds, residual, local_inverse, corner_basis, corner_map, coarse_inverse)


def solution(mesh):
    in_specs = (
        P(None, "sub", "grp", None),
        P(),
        P("sub", "grp", None, None),
        P("sub", "grp", None, None),
        P("sub", "grp", None),
        P(("sub", "grp"), None),
    )
    out_specs = (P(None, None, "sub", "grp", None), P())
    run = functools.partial(body, mesh.shape["sub"], mesh.shape["grp"])
    return jax.shard_map(run, mesh=mesh, in_specs=in_specs, out_specs=out_specs, check_vma=False)
```

```python
import functools

import jax
import jax.numpy as jnp
from jax import lax
from jax.experimental import pallas as pl
from jax.experimental.pallas import tpu as pltpu
from jax.sharding import PartitionSpec as P

S_STEP = 2
BLOCKS = 2 * S_STEP + 1
LEVELS = 2 * S_STEP
MESH = pl.DeviceIdType.MESH
HIGHEST = lax.Precision.HIGHEST


def exact(a, b):
    return jnp.dot(a, b, precision=HIGHEST, preferred_element_type=jnp.float32)


def across_rows(a, b, precision=None):
    return lax.dot_general(
        a, b, (((1,), (1,)), ((), ())), precision=precision, preferred_element_type=jnp.float32
    )


def dot(a, b):
    return jnp.dot(a, b, preferred_element_type=jnp.float32)


def kernel(
    nsub, ngrp, inner,
    bounds_hbm, res_hbm, inv_hbm, corner_hbm, map_hbm, coarse_hbm,
    basis_hbm, gram_hbm,
    basis_ref, gram_ref, bounds, res, inv, corner, ids_ref, up_out, up_in, low_out, low_in, term_out, term_in, edge,
    rows_c, near, far, high, rest, lift_high, lift_rest,
    load_sem, store_sem, up_send, up_recv, low_send, low_recv, term_send, term_recv, edge_send, edge_recv,
    rows_send, rows_recv, near_send, near_recv, far_send, far_recv,
):
    right, half = up_out.shape[2], high.shape[1]
    face = half // 2
    order = BLOCKS * right
    nco = rows_c.shape[3]
    planes = nsub // inner
    members = inner * ngrp
    sub = lax.axis_index("sub")
    grp = lax.axis_index("grp")
    plane = lax.div(sub, inner)
    within = lax.rem(sub, inner)
    member = within * ngrp + grp
    next_sub = (lax.rem(sub + 1, nsub), grp)
    prev_sub = (lax.rem(sub + nsub - 1, nsub), grp)
    next_grp = (sub, lax.rem(grp + 1, ngrp))
    prev_grp = (sub, lax.rem(grp + ngrp - 1, ngrp))

    def near_peer(offset):
        other = lax.rem(member + offset, members)
        return (plane * inner + lax.div(other, ngrp), lax.rem(other, ngrp))

    def far_peer(offset):
        return (lax.rem(plane + offset, planes) * inner + within, grp)

    near_peers = [near_peer(o) for o in range(1, members)]
    far_peers = [far_peer(o) for o in range(1, planes)]

    barrier = pltpu.get_barrier_semaphore()
    greeted = [next_sub, prev_sub] + far_peers + near_peers
    for peer in greeted:
        pl.semaphore_signal(barrier, inc=1, device_id=peer, device_id_type=MESH)

    loads = [
        pltpu.make_async_copy(src, dst, load_sem.at[i])
        for i, (src, dst) in enumerate((
            (corner_hbm, corner),
            (map_hbm, ids_ref),
            (res_hbm, res),
            (coarse_hbm, rows_c.at[plane, member]),
            (bounds_hbm, bounds),
            (inv_hbm.at[0, 0], inv),
        ))
    ]
    for copy in loads:
        copy.start()

    def send(src, dst, send_sem, recv_sem, peer):
        copy = pltpu.make_async_remote_copy(
            src_ref=src, dst_ref=dst, send_sem=send_sem, recv_sem=recv_sem,
            device_id=peer, device_id_type=MESH,
        )
        copy.start()
        return copy

    pending = []
    stores = []

    def landed(buf, count, send_sem, recv_sem, peer):
        part = buf.at[pl.ds(0, count - 1)]
        copy = pltpu.make_async_remote_copy(
            src_ref=part, dst_ref=part, send_sem=send_sem, recv_sem=recv_sem,
            device_id=peer, device_id_type=MESH,
        )
        copy.wait_recv()
        pending.append(copy)

    def split(value):
        rough = value.astype(jnp.bfloat16)
        return rough, (value - rough.astype(jnp.float32)).astype(jnp.bfloat16)

    def start_near(level, message):
        near[level, member] = message
        own = near.at[level, member]
        for peer in near_peers:
            send(own, own, near_send.at[level], near_recv.at[level], peer)

    def pass_far(level):
        landed(near.at[level], members, near_send.at[level], near_recv.at[level], near_peers[0])
        total = near[level, 0]
        for i in range(1, members):
            total = total + near[level, i]
        far[level, plane] = total
        own = far.at[level, plane]
        for peer in far_peers:
            send(own, own, far_send.at[level], far_recv.at[level], peer)

    def finish(level):
        landed(far.at[level], planes, far_send.at[level], far_recv.at[level], far_peers[0])
        total = far[level, 0]
        for i in range(1, planes):
            total = total + far[level, i]
        return total

    high[...] = jnp.zeros_like(high)
    rest[...] = jnp.zeros_like(rest)
    lift_high[...] = jnp.zeros_like(lift_high)
    lift_rest[...] = jnp.zeros_like(lift_rest)
    loads[0].wait()
    loads[1].wait()
    ids = ids_ref[0]
    table = (lax.broadcasted_iota(jnp.int32, (nco, ids.shape[1]), 0) == ids).astype(jnp.bfloat16)
    terms = dot(table, corner[0, 0])
    term_out[0] = terms[:, face : 2 * face]
    term_out[1] = terms[:, 3 * face :]
    for copy in loads[2:5]:
        copy.wait()
    x = res[:, 0, 0, :]
    centre = (bounds[0] + bounds[1]) / 2.0
    radius = (bounds[1] - bounds[0]) / 2.0
    scale = 1.0 / jnp.full((right, half), radius, jnp.float32)
    lane = lax.broadcasted_iota(jnp.int32, (right, high.shape[0]), 1)
    of_gram = lane < order

    def message(level, packed, remainder):
        both = across_rows(jnp.concatenate([packed, remainder], axis=0), high[...])
        second = across_rows(packed, rest[...])
        return both[:right] + (second + jnp.where(of_gram, both[right:], 0.0))

    def keep(level, value):
        packed, remainder = split(value)
        basis_ref[level, :, 0, 0, :] = value
        stores.append(pltpu.make_async_copy(basis_ref.at[level], basis_hbm.at[level], store_sem.at[level]))
        stores[-1].start()
        high[pl.ds(level * right, right), :] = packed
        rest[pl.ds(level * right, right), :] = remainder
        return packed, remainder

    pl.semaphore_wait(barrier, len(greeted))
    term_copies = [
        send(term_out.at[d], term_in.at[d], term_send.at[d], term_recv.at[d], peer)
        for d, peer in enumerate((prev_sub, prev_grp))
    ]
    pending += term_copies

    gram_rows = []
    previous = None
    for level in range(LEVELS):
        packed = x.astype(jnp.bfloat16)
        x_sub, x_grp = packed[:, :face], packed[:, face:]
        up_out[level, 0] = x_sub
        up_out[level, 1] = x_grp
        ups = [
            send(up_out.at[level, d], up_in.at[level, d], up_send.at[level, d], up_recv.at[level, d], peer)
            for d, peer in enumerate((next_sub, next_grp))
        ]
        pending += ups
        packed, remainder = keep(level, x)
        if level > 0:
            start_near(level, message(level, packed, remainder))
        else:
            own = rows_c.at[plane, member]
            for peer in near_peers:
                send(own, own, rows_send.at[0], rows_recv.at[0], peer)
            loads[5].wait()
            edges = [
                send(
                    inv.at[pl.ds(first, face), pl.ds(first, face)], edge.at[d],
                    edge_send.at[d], edge_recv.at[d], peer,
                )
                for d, (first, peer) in enumerate(((face, prev_sub), (3 * face, prev_grp)))
            ]
            pending += edges

        def own_part(first):
            columns = slice(first, first + face)
            return dot(x_sub, inv[:face, columns]) + dot(x_grp, inv[2 * face : 3 * face, columns])

        def low_part(value, row, first):
            return dot(value, inv[row : row + face, first : first + face])

        def send_low(d, value, peer):
            low_out[level, d] = value
            copy = send(
                low_out.at[level, d], low_in.at[level, d], low_send.at[level, d], low_recv.at[level, d], peer
            )
            pending.append(copy)
            return copy

        own_low = own_part(face)
        ups[1].wait_recv()
        low_grp = up_in[level, 1]
        from_sub = send_low(0, own_low - low_part(low_grp, 3 * face, face), prev_sub)
        own_low = own_part(3 * face)
        up_sub = own_part(0) - low_part(low_grp, 3 * face, 0)
        up_grp = own_part(2 * face) - low_part(low_grp, 3 * face, 2 * face)
        if level == 0:
            for copy in term_copies:
                copy.wait_recv()
            weight = jnp.concatenate(
                [terms[:, :face] - term_in[0], terms[:, 2 * face : 3 * face] - term_in[1]], axis=1
            )
            weight_high, weight_rest = split(weight)
            high[order : order + nco, :] = weight_high
            rest[order : order + nco, :] = weight_rest
            start_near(level, message(level, packed, remainder))
            landed(rows_c.at[plane], members, rows_send.at[0], rows_recv.at[0], near_peers[0])
            mine = rows_c.at[plane]
            for peer in far_peers:
                send(mine, mine, rows_send.at[1], rows_recv.at[1], peer)
        else:
            pass_far(level)
        ups[0].wait_recv()
        low_sub = up_in[level, 0]
        from_grp = send_low(1, own_low - low_part(low_sub, face, 3 * face), prev_grp)
        up_sub = up_sub - low_part(low_sub, face, 0)
        up_grp = up_grp - low_part(low_sub, face, 2 * face)
        if level == 0:
            pass_far(level)
            landed(rows_c, planes, rows_send.at[1], rows_recv.at[1], far_peers[0])
            raised = exact(rows_c[...].reshape(nco, nco), weight)
            raised_high, raised_rest = split(raised)
            lift_high[order : order + nco, :] = raised_high
            lift_rest[order : order + nco, :] = raised_rest
            for copy in edges:
                copy.wait_recv()
        up_sub = up_sub + dot(x_sub, edge[0])
        up_grp = up_grp + dot(x_grp, edge[1])
        base = jnp.concatenate([up_sub, up_grp], axis=1) - centre * x
        total = finish(level)
        gram_rows.append(total)
        total_high, total_rest = split(total)
        both = dot(jnp.concatenate([total_high, total_rest], axis=0), lift_high[...])
        image = base + (both[:right] + (both[right:] + dot(total_high, lift_rest[...])))
        from_sub.wait_recv()
        from_grp.wait_recv()
        image = image - jnp.concatenate([low_in[level, 0], low_in[level, 1]], axis=1)
        following = image * scale if level == 0 else 2.0 * image * scale - previous
        previous, x = x, following

    packed, remainder = keep(LEVELS, x)
    start_near(LEVELS, message(LEVELS, packed, remainder))
    pass_far(LEVELS)
    gram_rows.append(finish(LEVELS))
    full = jnp.concatenate(gram_rows, axis=0)[:, :order]
    row = lax.broadcasted_iota(jnp.int32, (order, order), 0)
    column = lax.broadcasted_iota(jnp.int32, (order, order), 1)
    below = jnp.where(lax.div(column, right) < lax.div(row, right), full, 0.0)
    same = jnp.where(lax.div(column, right) == lax.div(row, right), full, 0.0)
    gram_ref[...] = (below + same + below.T) * (1.0 / (half * nsub))
    stores.append(pltpu.make_async_copy(gram_ref, gram_hbm, store_sem.at[BLOCKS]))
    stores[-1].start()
    for copy in pending:
        copy.wait_send()
    for copy in stores:
        copy.wait()


def body(nsub, ngrp, residual, bounds, local_inverse, corner_basis, corner_map, coarse_inverse):
    right, half = residual.shape[0], residual.shape[3]
    face = half // 2
    width = 4 * face
    rows, nco = coarse_inverse.shape
    order = BLOCKS * right
    inner = 1
    while nsub % (2 * inner) == 0 and 2 * inner * ngrp <= nsub // inner:
        inner *= 2
    planes, members = nsub // inner, inner * ngrp
    wide = -(-(order + nco) // 128) * 128
    hbm = pl.BlockSpec(memory_space=pltpu.HBM)
    dma = pltpu.SemaphoreType.DMA
    f32, bf16 = jnp.float32, jnp.bfloat16
    return pl.pallas_call(
        functools.partial(kernel, nsub, ngrp, inner),
        out_shape=(
            jax.ShapeDtypeStruct((BLOCKS, right, 1, 1, half), f32),
            jax.ShapeDtypeStruct((order, order), f32),
        ),
        in_specs=[hbm] * 6,
        out_specs=(hbm, hbm),
        scratch_shapes=[
            pltpu.VMEM((BLOCKS, right, 1, 1, half), f32),
            pltpu.VMEM((order, order), f32),
            pltpu.SMEM(bounds.shape, f32),
            pltpu.VMEM(residual.shape, f32),
            pltpu.VMEM((width, width), bf16),
            pltpu.VMEM(corner_basis.shape, bf16),
            pltpu.VMEM(corner_map.shape, corner_map.dtype),
            pltpu.VMEM((LEVELS, 2, right, face), bf16),
            pltpu.VMEM((LEVELS, 2, right, face), bf16),
            pltpu.VMEM((LEVELS, 2, right, face), f32),
            pltpu.VMEM((LEVELS, 2, right, face), f32),
            pltpu.VMEM((2, nco, face), f32),
            pltpu.VMEM((2, nco, face), f32),
            pltpu.VMEM((2, face, face), bf16),
            pltpu.VMEM((planes, members, rows, nco), f32),
            pltpu.VMEM((BLOCKS, members, right, wide), f32),
            pltpu.VMEM((BLOCKS, planes, right, wide), f32),
            pltpu.VMEM((wide, half), bf16),
            pltpu.VMEM((wide, half), bf16),
            pltpu.VMEM((wide, half), bf16),
            pltpu.VMEM((wide, half), bf16),
            dma((6,)),
            dma((BLOCKS + 1,)),
            dma((LEVELS, 2)),
            dma((LEVELS, 2)),
            dma((LEVELS, 2)),
            dma((LEVELS, 2)),
            dma((2,)),
            dma((2,)),
            dma((2,)),
            dma((2,)),
            dma((2,)),
            dma((2,)),
            dma((BLOCKS,)),
            dma((BLOCKS,)),
            dma((BLOCKS,)),
            dma((BLOCKS,)),
        ],
        compiler_params=pltpu.CompilerParams(
            collective_id=0, has_side_effects=True, vmem_limit_bytes=60 * 1024 * 1024
        ),
    )(bounds, residual, local_inverse, corner_basis, corner_map, coarse_inverse)


def solution(mesh):
    in_specs = (
        P(None, "sub", "grp", None),
        P(),
        P("sub", "grp", None, None),
        P("sub", "grp", None, None),
        P("sub", "grp", None),
        P(("sub", "grp"), None),
    )
    out_specs = (P(None, None, "sub", "grp", None), P())
    run = functools.partial(body, mesh.shape["sub"], mesh.shape["grp"])
    return jax.shard_map(run, mesh=mesh, in_specs=in_specs, out_specs=out_specs, check_vma=False)
```

```python
import functools

import jax
import jax.numpy as jnp
from jax import lax
from jax.experimental import pallas as pl
from jax.experimental.pallas import tpu as pltpu
from jax.sharding import PartitionSpec as P

S_STEP = 2
BLOCKS = 2 * S_STEP + 1
LEVELS = 2 * S_STEP
MESH = pl.DeviceIdType.MESH
HIGHEST = lax.Precision.HIGHEST


def exact(a, b):
    return jnp.dot(a, b, precision=HIGHEST, preferred_element_type=jnp.float32)


def across_rows(a, b, precision=None):
    return lax.dot_general(
        a, b, (((1,), (1,)), ((), ())), precision=precision, preferred_element_type=jnp.float32
    )


def dot(a, b):
    return jnp.dot(a, b, preferred_element_type=jnp.float32)


def kernel(
    nsub, ngrp, inner, pack,
    bounds_hbm, res_hbm, inv_hbm, corner_hbm, map_hbm, coarse_hbm,
    basis_hbm, gram_hbm,
    basis_ref, gram_ref, bounds, res, inv, corner, ids_ref,
    up_out, up_in, diag_in, low_out, low_in, term_out, term_in, edge, cross,
    rows_c, direct, part_out, part_near, part_far, part_all, near, far,
    high, rest, load_high, load_rest, lift_high, lift_rest,
    load_sem, store_sem, up_send, up_recv, diag_send, diag_recv, low_send, low_recv,
    term_send, term_recv, edge_send, edge_recv, rows_send, rows_recv, direct_send, direct_recv,
    part_send, part_recv, near_send, near_recv, far_send, far_recv,
):
    right, half = up_out.shape[2], high.shape[1]
    face = half // 2
    order = BLOCKS * right
    nco = rows_c.shape[2]
    planes = nsub // inner
    members = inner * ngrp
    devices = nsub * ngrp
    packed_rows = right // pack
    chunk = part_out.shape[1]
    sub = lax.axis_index("sub")
    grp = lax.axis_index("grp")
    me = sub * ngrp + grp
    plane = lax.div(sub, inner)
    within = lax.rem(sub, inner)
    member = within * ngrp + grp
    sub_up, sub_down = lax.rem(sub + 1, nsub), lax.rem(sub + nsub - 1, nsub)
    grp_up, grp_down = lax.rem(grp + 1, ngrp), lax.rem(grp + ngrp - 1, ngrp)
    next_sub, prev_sub = (sub_up, grp), (sub_down, grp)
    next_grp, prev_grp = (sub, grp_up), (sub, grp_down)

    def any_peer(offset):
        other = lax.rem(me + offset, devices)
        return (lax.div(other, ngrp), lax.rem(other, ngrp))

    def to_all(action):
        def step(offset, carry):
            action(any_peer(offset))
            return carry

        lax.fori_loop(1, devices, step, 0)

    near_others = [lax.rem(member + o, members) for o in range(1, members)]
    near_peers = [(plane * inner + lax.div(o, ngrp), lax.rem(o, ngrp)) for o in near_others]
    far_peers = [(lax.rem(plane + o, planes) * inner + within, grp) for o in range(1, planes)]

    barrier = pltpu.get_barrier_semaphore()
    loads = [
        pltpu.make_async_copy(src, dst, load_sem.at[i])
        for i, (src, dst) in enumerate((
            (corner_hbm, corner),
            (map_hbm, ids_ref),
            (res_hbm, res),
            (coarse_hbm, rows_c.at[me]),
            (bounds_hbm, bounds),
            (inv_hbm.at[0, 0], inv),
        ))
    ]
    for copy in loads:
        copy.start()
    to_all(lambda peer: pl.semaphore_signal(barrier, inc=1, device_id=peer, device_id_type=MESH))

    def send(src, dst, send_sem, recv_sem, peer):
        copy = pltpu.make_async_remote_copy(
            src_ref=src, dst_ref=dst, send_sem=send_sem, recv_sem=recv_sem,
            device_id=peer, device_id_type=MESH,
        )
        copy.start()
        return copy

    pending = []
    stores = []

    def landed(buf, count, send_sem, recv_sem, peer):
        part = buf.at[pl.ds(0, count - 1)]
        copy = pltpu.make_async_remote_copy(
            src_ref=part, dst_ref=part, send_sem=send_sem, recv_sem=recv_sem,
            device_id=peer, device_id_type=MESH,
        )
        copy.wait_recv()
        pending.append(copy)

    def split(value):
        rough = value.astype(jnp.bfloat16)
        return rough, (value - rough.astype(jnp.float32)).astype(jnp.bfloat16)

    def added(buf, count):
        total = buf[0]
        for i in range(1, count):
            total = total + buf[i]
        return total

    def broadcast(buf, slot, peers, send_sem, recv_sem):
        own = buf.at[slot]
        for peer in peers:
            send(own, own, send_sem, recv_sem, peer)

    high[...] = jnp.zeros_like(high)
    rest[...] = jnp.zeros_like(rest)
    loads[0].wait()
    loads[1].wait()
    ids = ids_ref[0]
    table = (lax.broadcasted_iota(jnp.int32, (nco, ids.shape[1]), 0) == ids).astype(jnp.bfloat16)
    terms = dot(table, corner[0, 0])
    term_out[0] = terms[:, face : 2 * face]
    term_out[1] = terms[:, 3 * face :]
    for copy in loads[2:5]:
        copy.wait()
    x = res[:, 0, 0, :]
    centre = (bounds[0] + bounds[1]) / 2.0
    radius = (bounds[1] - bounds[0]) / 2.0
    scale = 1.0 / jnp.full((right, half), radius, jnp.float32)
    lane = lax.broadcasted_iota(jnp.int32, (right, pack * nco), 1)
    row = lax.broadcasted_iota(jnp.int32, (right, pack * nco), 0)
    mine = lax.div(lane, nco) == lax.div(row, packed_rows)

    def gram_part(first, second):
        both = across_rows(jnp.concatenate([first, second], axis=0), high[...])
        count = first.shape[0]
        return both[:count] + (both[count:] + across_rows(first, rest[...]))

    def coarse_part(packed):
        part = across_rows(packed, load_high[...]) + across_rows(packed, load_rest[...])
        if pack == 1:
            return part
        part = jnp.where(mine, part, 0.0)
        total = part[:packed_rows]
        for q in range(1, pack):
            total = total + part[q * packed_rows : (q + 1) * packed_rows]
        return total

    def coarse_lift(total):
        if pack > 1:
            total = jnp.where(mine, jnp.concatenate([total] * pack, axis=0), 0.0)
        total_high, total_rest = split(total)
        both = dot(jnp.concatenate([total_high, total_rest], axis=0), lift_high[...])
        return both[:right] + (both[right:] + dot(total_high, lift_rest[...]))

    def send_coarse(level, part):
        direct[level, me] = part
        own = direct.at[level, me]
        to_all(lambda peer: send(own, own, direct_send.at[level], direct_recv.at[level], peer))

    def keep(level, value):
        packed, remainder = split(value)
        basis_ref[level, :, 0, 0, :] = value
        high[pl.ds(level * right, right), :] = packed
        rest[pl.ds(level * right, right), :] = remainder
        stores.append(pltpu.make_async_copy(basis_ref.at[level], basis_hbm.at[level], store_sem.at[level]))
        stores[-1].start()
        return packed, remainder

    pl.semaphore_wait(barrier, devices - 1)
    term_copies = [
        send(term_out.at[d], term_in.at[d], term_send.at[d], term_recv.at[d], peer)
        for d, peer in enumerate((prev_sub, prev_grp))
    ]
    pending += term_copies

    previous = None
    for level in range(LEVELS):
        packed = x.astype(jnp.bfloat16)
        x_sub, x_grp = packed[:, :face], packed[:, face:]
        up_out[level, 0] = x_sub
        up_out[level, 1] = x_grp
        ups = [
            send(up_out.at[level, d], up_in.at[level, d], up_send.at[level, d], up_recv.at[level, d], peer)
            for d, peer in enumerate((next_sub, next_grp))
        ]
        diags = [
            send(up_out.at[level, d], diag_in.at[level, d], diag_send.at[level, d], diag_recv.at[level, d], peer)
            for d, peer in enumerate(((sub_up, grp_down), (sub_down, grp_up)))
        ]
        pending += ups + diags
        if level == 0:
            loads[5].wait()
        else:
            part = coarse_part(packed)

        def own_part(first):
            columns = slice(first, first + face)
            return dot(x_sub, inv[:face, columns]) + dot(x_grp, inv[2 * face : 3 * face, columns])

        def low_part(value, first, column):
            return dot(value, inv[first : first + face, column : column + face])

        low_out[level, 0] = own_part(face)
        low_out[level, 1] = own_part(3 * face)
        lows = [
            send(low_out.at[level, d], low_in.at[level, d], low_send.at[level, d], low_recv.at[level, d], peer)
            for d, peer in enumerate((prev_sub, prev_grp))
        ]
        pending += lows
        if level == 0:
            own = rows_c.at[me]
            to_all(lambda peer: send(own, own, rows_send, rows_recv, peer))
            blocks = [
                send(
                    inv.at[pl.ds(first, face), pl.ds(column, face)], landing.at[d],
                    edge_send.at[i], edge_recv.at[i], peer,
                )
                for i, (first, column, landing, d, peer) in enumerate((
                    (face, face, edge, 0, prev_sub),
                    (3 * face, 3 * face, edge, 1, prev_grp),
                    (3 * face, face, cross, 0, prev_sub),
                    (face, 3 * face, cross, 1, prev_grp),
                ))
            ]
            pending += blocks
            for copy in term_copies:
                copy.wait_recv()
            weight = jnp.concatenate(
                [terms[:, :face] - term_in[0], terms[:, 2 * face : 3 * face] - term_in[1]], axis=1
            )
            weight_high, weight_rest = split(weight)
            load_high[...] = jnp.concatenate([weight_high] * pack, axis=0)
            load_rest[...] = jnp.concatenate([weight_rest] * pack, axis=0)
            part = coarse_part(packed)
        send_coarse(level, part)
        packed, remainder = keep(level, x)
        if level == LEVELS - 1:
            count = LEVELS * right
            first_rows = gram_part(high[:count, :], rest[:count, :])
            for m in range(members):
                part_out[m] = first_rows[m * chunk : (m + 1) * chunk]
            part_near[member] = part_out[member]
            for other, peer in zip(near_others, near_peers):
                send(part_out.at[other], part_near.at[member], part_send.at[0], part_recv.at[0], peer)
        up_sub = own_part(0)
        up_grp = own_part(2 * face)
        for copy in ups:
            copy.wait_recv()
        low_sub, low_grp = up_in[level, 0], up_in[level, 1]
        up_sub = up_sub - low_part(low_sub, face, 0) - low_part(low_grp, 3 * face, 0)
        up_grp = up_grp - low_part(low_sub, face, 2 * face) - low_part(low_grp, 3 * face, 2 * face)
        if level == 0:
            landed(rows_c, devices, rows_send, rows_recv, next_grp)
            raised = exact(rows_c[...].reshape(nco, nco), weight)
            raised_high, raised_rest = split(raised)
            lift_high[...] = jnp.concatenate([raised_high] * pack, axis=0)
            lift_rest[...] = jnp.concatenate([raised_rest] * pack, axis=0)
            for copy in blocks:
                copy.wait_recv()
        up_sub = up_sub + dot(x_sub, edge[0])
        up_grp = up_grp + dot(x_grp, edge[1])
        for copy in diags:
            copy.wait_recv()
        up_sub = up_sub + dot(diag_in[level, 1], cross[0])
        up_grp = up_grp + dot(diag_in[level, 0], cross[1])
        base = jnp.concatenate([up_sub, up_grp], axis=1) - centre * x
        for copy in lows:
            copy.wait_recv()
        base = base - jnp.concatenate([low_in[level, 0], low_in[level, 1]], axis=1)
        landed(direct.at[level], devices, direct_send.at[level], direct_recv.at[level], next_grp)
        image = base + coarse_lift(added(direct.at[level], devices))
        following = image * scale if level == 0 else 2.0 * image * scale - previous
        previous, x = x, following

    packed, remainder = keep(LEVELS, x)
    near[member] = gram_part(packed, remainder)
    broadcast(near, member, near_peers, near_send, near_recv)
    landed(part_near, members, part_send.at[0], part_recv.at[0], near_peers[0])
    part_far[plane] = added(part_near, members)
    broadcast(part_far, plane, far_peers, part_send.at[1], part_recv.at[1])
    landed(near, members, near_send, near_recv, near_peers[0])
    far[plane] = added(near, members)
    broadcast(far, plane, far_peers, far_send, far_recv)
    landed(part_far, planes, part_send.at[1], part_recv.at[1], far_peers[0])
    part_all[member] = added(part_far, planes)
    broadcast(part_all, member, near_peers, part_send.at[2], part_recv.at[2])
    landed(far, planes, far_send, far_recv, far_peers[0])
    last_rows = added(far, planes)
    landed(part_all, members, part_send.at[2], part_recv.at[2], near_peers[0])
    full = jnp.concatenate([part_all[m] for m in range(members)] + [last_rows], axis=0)[:, :order]
    row = lax.broadcasted_iota(jnp.int32, (order, order), 0)
    column = lax.broadcasted_iota(jnp.int32, (order, order), 1)
    below = jnp.where(lax.div(column, right) < lax.div(row, right), full, 0.0)
    same = jnp.where(lax.div(column, right) == lax.div(row, right), full, 0.0)
    gram_ref[...] = (below + same + below.T) * (1.0 / (half * nsub))
    stores.append(pltpu.make_async_copy(gram_ref, gram_hbm, store_sem.at[BLOCKS]))
    stores[-1].start()
    for copy in pending:
        copy.wait_send()
    for copy in stores:
        copy.wait()


def body(nsub, ngrp, residual, bounds, local_inverse, corner_basis, corner_map, coarse_inverse):
    right, half = residual.shape[0], residual.shape[3]
    face = half // 2
    width = 4 * face
    rows, nco = coarse_inverse.shape
    order = BLOCKS * right
    devices = nsub * ngrp
    inner = 1
    while nsub % (2 * inner) == 0 and 2 * inner * ngrp <= nsub // inner:
        inner *= 2
    planes, members = nsub // inner, inner * ngrp
    wide = -(-order // 128) * 128
    pack = 128 // nco if nco < 128 and 128 % nco == 0 and right % (128 // nco) == 0 else 1
    lanes = pack * nco
    chunk = LEVELS * right // members
    hbm = pl.BlockSpec(memory_space=pltpu.HBM)
    dma = pltpu.SemaphoreType.DMA
    f32, bf16 = jnp.float32, jnp.bfloat16
    return pl.pallas_call(
        functools.partial(kernel, nsub, ngrp, inner, pack),
        out_shape=(
            jax.ShapeDtypeStruct((BLOCKS, right, 1, 1, half), f32),
            jax.ShapeDtypeStruct((order, order), f32),
        ),
        in_specs=[hbm] * 6,
        out_specs=(hbm, hbm),
        scratch_shapes=[
            pltpu.VMEM((BLOCKS, right, 1, 1, half), f32),
            pltpu.VMEM((order, order), f32),
            pltpu.SMEM(bounds.shape, f32),
            pltpu.VMEM(residual.shape, f32),
            pltpu.VMEM((width, width), bf16),
            pltpu.VMEM(corner_basis.shape, bf16),
            pltpu.VMEM(corner_map.shape, corner_map.dtype),
            pltpu.VMEM((LEVELS, 2, right, face), bf16),
            pltpu.VMEM((LEVELS, 2, right, face), bf16),
            pltpu.VMEM((LEVELS, 2, right, face), bf16),
            pltpu.VMEM((LEVELS, 2, right, face), f32),
            pltpu.VMEM((LEVELS, 2, right, face), f32),
            pltpu.VMEM((2, nco, face), f32),
            pltpu.VMEM((2, nco, face), f32),
            pltpu.VMEM((2, face, face), bf16),
            pltpu.VMEM((2, face, face), bf16),
            pltpu.VMEM((devices, rows, nco), f32),
            pltpu.VMEM((LEVELS, devices, right // pack, lanes), f32),
            pltpu.VMEM((members, chunk, wide), f32),
            pltpu.VMEM((members, chunk, wide), f32),
            pltpu.VMEM((planes, chunk, wide), f32),
            pltpu.VMEM((members, chunk, wide), f32),
            pltpu.VMEM((members, right, wide), f32),
            pltpu.VMEM((planes, right, wide), f32),
            pltpu.VMEM((wide, half), bf16),
            pltpu.VMEM((wide, half), bf16),
            pltpu.VMEM((lanes, half), bf16),
            pltpu.VMEM((lanes, half), bf16),
            pltpu.VMEM((lanes, half), bf16),
            pltpu.VMEM((lanes, half), bf16),
            dma((6,)),
            dma((BLOCKS + 1,)),
            dma((LEVELS, 2)),
            dma((LEVELS, 2)),
            dma((LEVELS, 2)),
            dma((LEVELS, 2)),
            dma((LEVELS, 2)),
            dma((LEVELS, 2)),
            dma((2,)),
            dma((2,)),
            dma((4,)),
            dma((4,)),
            dma,
            dma,
            dma((LEVELS,)),
            dma((LEVELS,)),
            dma((3,)),
            dma((3,)),
            dma,
            dma,
            dma,
            dma,
        ],
        compiler_params=pltpu.CompilerParams(
            collective_id=0, has_side_effects=True, vmem_limit_bytes=60 * 1024 * 1024
        ),
    )(bounds, residual, local_inverse, corner_basis, corner_map, coarse_inverse)


def solution(mesh):
    in_specs = (
        P(None, "sub", "grp", None),
        P(),
        P("sub", "grp", None, None),
        P("sub", "grp", None, None),
        P("sub", "grp", None),
        P(("sub", "grp"), None),
    )
    out_specs = (P(None, None, "sub", "grp", None), P())
    run = functools.partial(body, mesh.shape["sub"], mesh.shape["grp"])
    return jax.shard_map(run, mesh=mesh, in_specs=in_specs, out_specs=out_specs, check_vma=False)
```

```python
import functools

import jax
import jax.numpy as jnp
from jax import lax
from jax.experimental import pallas as pl
from jax.experimental.pallas import tpu as pltpu
from jax.sharding import PartitionSpec as P

S_STEP = 2
BLOCKS = 2 * S_STEP + 1
LEVELS = 2 * S_STEP
LOGICAL = pl.DeviceIdType.LOGICAL
HIGHEST = lax.Precision.HIGHEST


def exact(a, b):
    return jnp.dot(a, b, precision=HIGHEST, preferred_element_type=jnp.float32)


def across_rows(a, b, precision=None):
    return lax.dot_general(
        a, b, (((1,), (1,)), ((), ())), precision=precision, preferred_element_type=jnp.float32
    )


def dot(a, b):
    return jnp.dot(a, b, preferred_element_type=jnp.float32)


def kernel(
    nsub, ngrp, inner, pack,
    bounds_hbm, res_hbm, inv_hbm, corner_hbm, map_hbm, coarse_hbm,
    basis_hbm, gram_hbm,
    basis_ref, gram_ref, bounds, res, inv, corner, ids_ref,
    up_out, up_in, diag_in, low_out, low_in, term_out, term_in, edge, cross,
    rows_c, direct, part_out, part_near, part_far, part_all, near, far,
    high, rest, load_high, load_rest, lift_high, lift_rest,
    load_sem, store_sem, up_send, up_recv, diag_send, diag_recv, low_send, low_recv,
    term_send, term_recv, edge_send, edge_recv, rows_send, rows_recv, direct_send, direct_recv,
    part_send, part_recv, near_send, near_recv, far_send, far_recv,
):
    right, half = up_out.shape[2], high.shape[1]
    face = half // 2
    order = BLOCKS * right
    nco = rows_c.shape[2]
    planes = nsub // inner
    members = inner * ngrp
    devices = nsub * ngrp
    packed_rows = right // pack
    chunk = part_out.shape[1]
    sub = lax.axis_index("sub")
    grp = lax.axis_index("grp")
    me = sub * ngrp + grp
    plane = lax.div(sub, inner)
    within = lax.rem(sub, inner)
    member = within * ngrp + grp
    sub_up, sub_down = lax.rem(sub + 1, nsub), lax.rem(sub + nsub - 1, nsub)
    grp_up, grp_down = lax.rem(grp + 1, ngrp), lax.rem(grp + ngrp - 1, ngrp)
    next_sub, prev_sub = sub_up * ngrp + grp, sub_down * ngrp + grp
    next_grp, prev_grp = sub * ngrp + grp_up, sub * ngrp + grp_down
    diagonal_peers = (sub_up * ngrp + grp_down, sub_down * ngrp + grp_up)

    def to_all(action):
        def step(offset, carry):
            other = me + offset
            action(jnp.where(other >= devices, other - devices, other))
            return carry

        lax.fori_loop(1, devices, step, 0)

    near_others = [lax.rem(member + o, members) for o in range(1, members)]
    near_peers = [plane * members + o for o in near_others]
    far_peers = [lax.rem(plane + o, planes) * members + member for o in range(1, planes)]

    barrier = pltpu.get_barrier_semaphore()
    loads = [
        pltpu.make_async_copy(src, dst, load_sem.at[i])
        for i, (src, dst) in enumerate((
            (corner_hbm, corner),
            (map_hbm, ids_ref),
            (res_hbm, res),
            (coarse_hbm, rows_c.at[me]),
            (bounds_hbm, bounds),
            (inv_hbm.at[0, 0], inv),
        ))
    ]
    for copy in loads:
        copy.start()
    to_all(lambda peer: pl.semaphore_signal(barrier, inc=1, device_id=peer, device_id_type=LOGICAL))

    def send(src, dst, send_sem, recv_sem, peer):
        copy = pltpu.make_async_remote_copy(
            src_ref=src, dst_ref=dst, send_sem=send_sem, recv_sem=recv_sem,
            device_id=peer, device_id_type=LOGICAL,
        )
        copy.start()
        return copy

    pending = []
    stores = []

    def landed(buf, count, send_sem, recv_sem, peer):
        part = buf.at[pl.ds(0, count - 1)]
        copy = pltpu.make_async_remote_copy(
            src_ref=part, dst_ref=part, send_sem=send_sem, recv_sem=recv_sem,
            device_id=peer, device_id_type=LOGICAL,
        )
        copy.wait_recv()
        pending.append(copy)

    def split(value):
        rough = value.astype(jnp.bfloat16)
        return rough, (value - rough.astype(jnp.float32)).astype(jnp.bfloat16)

    def added(buf, count):
        total = buf[0]
        for i in range(1, count):
            total = total + buf[i]
        return total

    def broadcast(buf, slot, peers, send_sem, recv_sem):
        own = buf.at[slot]
        for peer in peers:
            send(own, own, send_sem, recv_sem, peer)

    high[...] = jnp.zeros_like(high)
    rest[...] = jnp.zeros_like(rest)
    loads[0].wait()
    loads[1].wait()
    ids = ids_ref[0]
    table = (lax.broadcasted_iota(jnp.int32, (nco, ids.shape[1]), 0) == ids).astype(jnp.bfloat16)
    terms = dot(table, corner[0, 0])
    term_out[0] = terms[:, face : 2 * face]
    term_out[1] = terms[:, 3 * face :]
    for copy in loads[2:5]:
        copy.wait()
    x = res[:, 0, 0, :]
    centre = (bounds[0] + bounds[1]) / 2.0
    radius = (bounds[1] - bounds[0]) / 2.0
    scale = 1.0 / jnp.full((right, half), radius, jnp.float32)
    lane = lax.broadcasted_iota(jnp.int32, (right, pack * nco), 1)
    row = lax.broadcasted_iota(jnp.int32, (right, pack * nco), 0)
    mine = lax.div(lane, nco) == lax.div(row, packed_rows)

    def gram_part(first, second):
        both = across_rows(jnp.concatenate([first, second], axis=0), high[...])
        count = first.shape[0]
        return both[:count] + (both[count:] + across_rows(first, rest[...]))

    def coarse_part(packed):
        part = across_rows(packed, load_high[...]) + across_rows(packed, load_rest[...])
        if pack == 1:
            return part
        part = jnp.where(mine, part, 0.0)
        total = part[:packed_rows]
        for q in range(1, pack):
            total = total + part[q * packed_rows : (q + 1) * packed_rows]
        return total

    def coarse_lift(total):
        if pack > 1:
            total = jnp.where(mine, jnp.concatenate([total] * pack, axis=0), 0.0)
        total_high, total_rest = split(total)
        both = dot(jnp.concatenate([total_high, total_rest], axis=0), lift_high[...])
        return both[:right] + (both[right:] + dot(total_high, lift_rest[...]))

    def send_coarse(level, part):
        direct[level, me] = part
        own = direct.at[level, me]
        to_all(lambda peer: send(own, own, direct_send.at[level], direct_recv.at[level], peer))

    def keep(level, value):
        packed, remainder = split(value)
        basis_ref[level, :, 0, 0, :] = value
        high[pl.ds(level * right, right), :] = packed
        rest[pl.ds(level * right, right), :] = remainder
        stores.append(pltpu.make_async_copy(basis_ref.at[level], basis_hbm.at[level], store_sem.at[level]))
        stores[-1].start()
        return packed, remainder

    pl.semaphore_wait(barrier, devices - 1)
    term_copies = [
        send(term_out.at[d], term_in.at[d], term_send.at[d], term_recv.at[d], peer)
        for d, peer in enumerate((prev_sub, prev_grp))
    ]
    pending += term_copies

    previous = None
    for level in range(LEVELS):
        packed = x.astype(jnp.bfloat16)
        x_sub, x_grp = packed[:, :face], packed[:, face:]
        up_out[level, 0] = x_sub
        up_out[level, 1] = x_grp
        ups = [
            send(up_out.at[level, d], up_in.at[level, d], up_send.at[level, d], up_recv.at[level, d], peer)
            for d, peer in enumerate((next_sub, next_grp))
        ]
        diags = [
            send(up_out.at[level, d], diag_in.at[level, d], diag_send.at[level, d], diag_recv.at[level, d], peer)
            for d, peer in enumerate(diagonal_peers)
        ] if level > 0 else []
        pending += ups + diags
        if level > 0:
            part = coarse_part(packed)
        else:
            own = rows_c.at[me]
            to_all(lambda peer: send(own, own, rows_send, rows_recv, peer))
            loads[5].wait()

        def own_part(first):
            columns = slice(first, first + face)
            return dot(x_sub, inv[:face, columns]) + dot(x_grp, inv[2 * face : 3 * face, columns])

        def low_part(value, first, column):
            return dot(value, inv[first : first + face, column : column + face])

        def send_lows(first, second):
            low_out[level, 0] = first.astype(low_out.dtype)
            low_out[level, 1] = second.astype(low_out.dtype)
            copies = [
                send(low_out.at[level, d], low_in.at[level, d], low_send.at[level, d], low_recv.at[level, d], peer)
                for d, peer in enumerate((prev_sub, prev_grp))
            ]
            pending.extend(copies)
            return copies

        first_low, second_low = own_part(face), own_part(3 * face)
        if level > 0:
            lows = send_lows(first_low, second_low)
        else:
            for copy in ups:
                copy.wait_recv()
            low_sub, low_grp = up_in[level, 0], up_in[level, 1]
            lows = send_lows(
                first_low - low_part(low_sub, face, face) - low_part(low_grp, 3 * face, face),
                second_low - low_part(low_sub, face, 3 * face) - low_part(low_grp, 3 * face, 3 * face),
            )
            for copy in term_copies:
                copy.wait_recv()
            weight = jnp.concatenate(
                [terms[:, :face] - term_in[0], terms[:, 2 * face : 3 * face] - term_in[1]], axis=1
            )
            weight_high, weight_rest = split(weight)
            load_high[...] = jnp.concatenate([weight_high] * pack, axis=0)
            load_rest[...] = jnp.concatenate([weight_rest] * pack, axis=0)
            part = coarse_part(packed)
        send_coarse(level, part)
        if level == 0:
            blocks = [
                send(
                    inv.at[pl.ds(first, face), pl.ds(column, face)], landing.at[d],
                    edge_send.at[i], edge_recv.at[i], peer,
                )
                for i, (first, column, landing, d, peer) in enumerate((
                    (face, face, edge, 0, prev_sub),
                    (3 * face, face, cross, 0, prev_sub),
                    (3 * face, 3 * face, edge, 1, prev_grp),
                    (face, 3 * face, cross, 1, prev_grp),
                ))
            ]
            pending += blocks
        packed, remainder = keep(level, x)
        if level == LEVELS - 1:
            count = LEVELS * right
            first_rows = gram_part(high[:count, :], rest[:count, :])
            for m in range(members):
                part_out[m] = first_rows[m * chunk : (m + 1) * chunk]
            part_near[member] = part_out[member]
            for other, peer in zip(near_others, near_peers):
                send(part_out.at[other], part_near.at[member], part_send.at[0], part_recv.at[0], peer)
        up_sub = own_part(0)
        up_grp = own_part(2 * face)
        if level > 0:
            for copy in ups:
                copy.wait_recv()
            low_sub, low_grp = up_in[level, 0], up_in[level, 1]
        up_sub = up_sub - low_part(low_sub, face, 0) - low_part(low_grp, 3 * face, 0)
        up_grp = up_grp - low_part(low_sub, face, 2 * face) - low_part(low_grp, 3 * face, 2 * face)
        if level == 0:
            landed(rows_c, devices, rows_send, rows_recv, next_grp)
            raised = exact(rows_c[...].reshape(nco, nco), weight)
            raised_high, raised_rest = split(raised)
            lift_high[...] = jnp.concatenate([raised_high] * pack, axis=0)
            lift_rest[...] = jnp.concatenate([raised_rest] * pack, axis=0)
        else:
            if level == 1:
                for copy in blocks:
                    copy.wait_recv()
            up_sub = up_sub + dot(x_sub, edge[0])
            up_grp = up_grp + dot(x_grp, edge[1])
            for copy in diags:
                copy.wait_recv()
            up_sub = up_sub + dot(diag_in[level, 1], cross[0])
            up_grp = up_grp + dot(diag_in[level, 0], cross[1])
        base = jnp.concatenate([up_sub, up_grp], axis=1) - centre * x
        for copy in lows:
            copy.wait_recv()
        base = base - jnp.concatenate([low_in[level, 0], low_in[level, 1]], axis=1).astype(jnp.float32)
        landed(direct.at[level], devices, direct_send.at[level], direct_recv.at[level], next_grp)
        image = base + coarse_lift(added(direct.at[level], devices))
        following = image * scale if level == 0 else 2.0 * image * scale - previous
        previous, x = x, following

    packed, remainder = keep(LEVELS, x)
    near[member] = gram_part(packed, remainder)
    broadcast(near, member, near_peers, near_send, near_recv)
    landed(part_near, members, part_send.at[0], part_recv.at[0], near_peers[0])
    part_far[plane] = added(part_near, members)
    broadcast(part_far, plane, far_peers, part_send.at[1], part_recv.at[1])
    landed(near, members, near_send, near_recv, near_peers[0])
    far[plane] = added(near, members)
    broadcast(far, plane, far_peers, far_send, far_recv)
    landed(part_far, planes, part_send.at[1], part_recv.at[1], far_peers[0])
    part_all[member] = added(part_far, planes)
    broadcast(part_all, member, near_peers, part_send.at[2], part_recv.at[2])
    landed(far, planes, far_send, far_recv, far_peers[0])
    last_rows = added(far, planes)
    landed(part_all, members, part_send.at[2], part_recv.at[2], near_peers[0])
    full = jnp.concatenate([part_all[m] for m in range(members)] + [last_rows], axis=0)[:, :order]
    row = lax.broadcasted_iota(jnp.int32, (order, order), 0)
    column = lax.broadcasted_iota(jnp.int32, (order, order), 1)
    below = jnp.where(lax.div(column, right) < lax.div(row, right), full, 0.0)
    same = jnp.where(lax.div(column, right) == lax.div(row, right), full, 0.0)
    gram_ref[...] = (below + same + below.T) * (1.0 / (half * nsub))
    stores.append(pltpu.make_async_copy(gram_ref, gram_hbm, store_sem.at[BLOCKS]))
    stores[-1].start()
    for copy in pending:
        copy.wait_send()
    for copy in stores:
        copy.wait()


def body(nsub, ngrp, residual, bounds, local_inverse, corner_basis, corner_map, coarse_inverse):
    right, half = residual.shape[0], residual.shape[3]
    face = half // 2
    width = 4 * face
    rows, nco = coarse_inverse.shape
    order = BLOCKS * right
    devices = nsub * ngrp
    inner = 1
    while nsub % (2 * inner) == 0 and 2 * inner * ngrp <= nsub // inner:
        inner *= 2
    planes, members = nsub // inner, inner * ngrp
    wide = -(-order // 128) * 128
    pack = 128 // nco if nco < 128 and 128 % nco == 0 and right % (128 // nco) == 0 else 1
    lanes = pack * nco
    chunk = LEVELS * right // members
    hbm = pl.BlockSpec(memory_space=pltpu.HBM)
    dma = pltpu.SemaphoreType.DMA
    f32, bf16 = jnp.float32, jnp.bfloat16
    return pl.pallas_call(
        functools.partial(kernel, nsub, ngrp, inner, pack),
        out_shape=(
            jax.ShapeDtypeStruct((BLOCKS, right, 1, 1, half), f32),
            jax.ShapeDtypeStruct((order, order), f32),
        ),
        in_specs=[hbm] * 6,
        out_specs=(hbm, hbm),
        scratch_shapes=[
            pltpu.VMEM((BLOCKS, right, 1, 1, half), f32),
            pltpu.VMEM((order, order), f32),
            pltpu.SMEM(bounds.shape, f32),
            pltpu.VMEM(residual.shape, f32),
            pltpu.VMEM((width, width), bf16),
            pltpu.VMEM(corner_basis.shape, bf16),
            pltpu.VMEM(corner_map.shape, corner_map.dtype),
            pltpu.VMEM((LEVELS, 2, right, face), bf16),
            pltpu.VMEM((LEVELS, 2, right, face), bf16),
            pltpu.VMEM((LEVELS, 2, right, face), bf16),
            pltpu.VMEM((LEVELS, 2, right, face), bf16),
            pltpu.VMEM((LEVELS, 2, right, face), bf16),
            pltpu.VMEM((2, nco, face), f32),
            pltpu.VMEM((2, nco, face), f32),
            pltpu.VMEM((2, face, face), bf16),
            pltpu.VMEM((2, face, face), bf16),
            pltpu.VMEM((devices, rows, nco), f32),
            pltpu.VMEM((LEVELS, devices, right // pack, lanes), f32),
            pltpu.VMEM((members, chunk, wide), f32),
            pltpu.VMEM((members, chunk, wide), f32),
            pltpu.VMEM((planes, chunk, wide), f32),
            pltpu.VMEM((members, chunk, wide), f32),
            pltpu.VMEM((members, right, wide), f32),
            pltpu.VMEM((planes, right, wide), f32),
            pltpu.VMEM((wide, half), bf16),
            pltpu.VMEM((wide, half), bf16),
            pltpu.VMEM((lanes, half), bf16),
            pltpu.VMEM((lanes, half), bf16),
            pltpu.VMEM((lanes, half), bf16),
            pltpu.VMEM((lanes, half), bf16),
            dma((6,)),
            dma((BLOCKS + 1,)),
            dma((LEVELS, 2)),
            dma((LEVELS, 2)),
            dma((LEVELS, 2)),
            dma((LEVELS, 2)),
            dma((LEVELS, 2)),
            dma((LEVELS, 2)),
            dma((2,)),
            dma((2,)),
            dma((4,)),
            dma((4,)),
            dma,
            dma,
            dma((LEVELS,)),
            dma((LEVELS,)),
            dma((3,)),
            dma((3,)),
            dma,
            dma,
            dma,
            dma,
        ],
        compiler_params=pltpu.CompilerParams(
            collective_id=0, has_side_effects=True, vmem_limit_bytes=60 * 1024 * 1024
        ),
    )(bounds, residual, local_inverse, corner_basis, corner_map, coarse_inverse)


def solution(mesh):
    in_specs = (
        P(None, "sub", "grp", None),
        P(),
        P("sub", "grp", None, None),
        P("sub", "grp", None, None),
        P("sub", "grp", None),
        P(("sub", "grp"), None),
    )
    out_specs = (P(None, None, "sub", "grp", None), P())
    run = functools.partial(body, mesh.shape["sub"], mesh.shape["grp"])
    return jax.shard_map(run, mesh=mesh, in_specs=in_specs, out_specs=out_specs, check_vma=False)
```

```python
import functools

import jax
import jax.numpy as jnp
from jax import lax
from jax.experimental import pallas as pl
from jax.experimental.pallas import tpu as pltpu
from jax.sharding import PartitionSpec as P

S_STEP = 2
BLOCKS = 2 * S_STEP + 1
LEVELS = 2 * S_STEP
LOGICAL = pl.DeviceIdType.LOGICAL
HIGHEST = lax.Precision.HIGHEST


def exact(a, b):
    return jnp.dot(a, b, precision=HIGHEST, preferred_element_type=jnp.float32)


def across_rows(a, b, precision=None):
    return lax.dot_general(
        a, b, (((1,), (1,)), ((), ())), precision=precision, preferred_element_type=jnp.float32
    )


def dot(a, b):
    return jnp.dot(a, b, preferred_element_type=jnp.float32)


def kernel(
    nsub, ngrp, inner, pack,
    bounds_hbm, res_hbm, inv_hbm, corner_hbm, map_hbm, coarse_hbm,
    basis_hbm, gram_hbm,
    basis_ref, gram_ref, bounds, res, inv, corner, ids_ref,
    up_out, up_in, diag_in, low_out, low_in, term_out, term_in, edge, cross,
    rows_c, direct, part_out, part_near, part_far, part_all, near, far,
    high, rest, load_high, load_rest, lift_high, lift_rest,
    load_sem, store_sem, up_send, up_recv, diag_send, diag_recv, low_send, low_recv,
    term_send, term_recv, edge_send, edge_recv, rows_send, rows_recv, direct_send, direct_recv,
    part_send, part_recv, near_send, near_recv, far_send, far_recv,
):
    right, half = up_out.shape[2], high.shape[1]
    face = half // 2
    order = BLOCKS * right
    nco = rows_c.shape[2]
    planes = nsub // inner
    members = inner * ngrp
    devices = nsub * ngrp
    packed_rows = right // pack
    chunk = part_out.shape[1]
    sub = lax.axis_index("sub")
    grp = lax.axis_index("grp")
    me = sub * ngrp + grp
    plane = lax.div(sub, inner)
    within = lax.rem(sub, inner)
    member = within * ngrp + grp
    sub_up, sub_down = lax.rem(sub + 1, nsub), lax.rem(sub + nsub - 1, nsub)
    grp_up, grp_down = lax.rem(grp + 1, ngrp), lax.rem(grp + ngrp - 1, ngrp)
    next_sub, prev_sub = sub_up * ngrp + grp, sub_down * ngrp + grp
    next_grp, prev_grp = sub * ngrp + grp_up, sub * ngrp + grp_down
    diagonal_peers = (sub_up * ngrp + grp_down, sub_down * ngrp + grp_up)

    def to_all(action):
        def step(offset, carry):
            other = me + offset
            action(jnp.where(other >= devices, other - devices, other))
            return carry

        lax.fori_loop(1, devices, step, 0, unroll=devices <= 64)

    near_others = [lax.rem(member + o, members) for o in range(1, members)]
    near_peers = [plane * members + o for o in near_others]
    far_peers = [lax.rem(plane + o, planes) * members + member for o in range(1, planes)]

    barrier = pltpu.get_barrier_semaphore()
    loads = [
        pltpu.make_async_copy(src, dst, load_sem.at[i])
        for i, (src, dst) in enumerate((
            (corner_hbm, corner),
            (map_hbm, ids_ref),
            (res_hbm, res),
            (coarse_hbm, rows_c.at[me]),
            (bounds_hbm, bounds),
            (inv_hbm.at[0, 0], inv),
        ))
    ]
    for copy in loads:
        copy.start()
    to_all(lambda peer: pl.semaphore_signal(barrier, inc=1, device_id=peer, device_id_type=LOGICAL))

    def send(src, dst, send_sem, recv_sem, peer):
        copy = pltpu.make_async_remote_copy(
            src_ref=src, dst_ref=dst, send_sem=send_sem, recv_sem=recv_sem,
            device_id=peer, device_id_type=LOGICAL,
        )
        copy.start()
        return copy

    pending = []
    stores = []

    def landed(buf, count, send_sem, recv_sem, peer):
        part = buf.at[pl.ds(0, count - 1)]
        copy = pltpu.make_async_remote_copy(
            src_ref=part, dst_ref=part, send_sem=send_sem, recv_sem=recv_sem,
            device_id=peer, device_id_type=LOGICAL,
        )
        copy.wait_recv()
        pending.append(copy)

    def split(value):
        rough = value.astype(jnp.bfloat16)
        return rough, (value - rough.astype(jnp.float32)).astype(jnp.bfloat16)

    def added(buf, count):
        total = buf[0]
        for i in range(1, count):
            total = total + buf[i]
        return total

    def broadcast(buf, slot, peers, send_sem, recv_sem):
        own = buf.at[slot]
        for peer in peers:
            send(own, own, send_sem, recv_sem, peer)

    high[...] = jnp.zeros_like(high)
    rest[...] = jnp.zeros_like(rest)
    loads[0].wait()
    loads[1].wait()
    ids = ids_ref[0]
    table = (lax.broadcasted_iota(jnp.int32, (nco, ids.shape[1]), 0) == ids).astype(jnp.bfloat16)
    terms = dot(table, corner[0, 0])
    term_out[0] = terms[:, face : 2 * face]
    term_out[1] = terms[:, 3 * face :]
    for copy in loads[2:5]:
        copy.wait()
    x = res[:, 0, 0, :]
    centre = (bounds[0] + bounds[1]) / 2.0
    radius = (bounds[1] - bounds[0]) / 2.0
    scale = 1.0 / jnp.full((right, half), radius, jnp.float32)
    lane = lax.broadcasted_iota(jnp.int32, (right, pack * nco), 1)
    row = lax.broadcasted_iota(jnp.int32, (right, pack * nco), 0)
    mine = lax.div(lane, nco) == lax.div(row, packed_rows)

    def gram_part(first, second):
        both = across_rows(jnp.concatenate([first, second], axis=0), high[...])
        count = first.shape[0]
        return both[:count] + (both[count:] + across_rows(first, rest[...]))

    def coarse_part(packed):
        part = across_rows(packed, load_high[...]) + across_rows(packed, load_rest[...])
        if pack == 1:
            return part
        part = jnp.where(mine, part, 0.0)
        total = part[:packed_rows]
        for q in range(1, pack):
            total = total + part[q * packed_rows : (q + 1) * packed_rows]
        return total

    def coarse_lift(total):
        if pack > 1:
            total = jnp.where(mine, jnp.concatenate([total] * pack, axis=0), 0.0)
        total_high, total_rest = split(total)
        both = dot(jnp.concatenate([total_high, total_rest], axis=0), lift_high[...])
        return both[:right] + (both[right:] + dot(total_high, lift_rest[...]))

    def send_coarse(level, part):
        direct[level, me] = part
        own = direct.at[level, me]
        to_all(lambda peer: send(own, own, direct_send.at[level], direct_recv.at[level], peer))

    def keep(level, value):
        packed, remainder = split(value)
        basis_ref[level, :, 0, 0, :] = value
        high[pl.ds(level * right, right), :] = packed
        rest[pl.ds(level * right, right), :] = remainder
        stores.append(pltpu.make_async_copy(basis_ref.at[level], basis_hbm.at[level], store_sem.at[level]))
        stores[-1].start()
        return packed, remainder

    pl.semaphore_wait(barrier, devices - 1)
    term_copies = [
        send(term_out.at[d], term_in.at[d], term_send.at[d], term_recv.at[d], peer)
        for d, peer in enumerate((prev_sub, prev_grp))
    ]
    pending += term_copies

    previous = None
    for level in range(LEVELS):
        packed = x.astype(jnp.bfloat16)
        x_sub, x_grp = packed[:, :face], packed[:, face:]
        up_out[level, 0] = x_sub
        up_out[level, 1] = x_grp
        ups = [
            send(up_out.at[level, d], up_in.at[level, d], up_send.at[level, d], up_recv.at[level, d], peer)
            for d, peer in enumerate((next_sub, next_grp))
        ]
        diags = [
            send(up_out.at[level, d], diag_in.at[level, d], diag_send.at[level, d], diag_recv.at[level, d], peer)
            for d, peer in enumerate(diagonal_peers)
        ]
        pending += ups + diags
        if level == 0:
            loads[5].wait()
        else:
            part = coarse_part(packed)

        def own_part(first):
            columns = slice(first, first + face)
            return dot(x_sub, inv[:face, columns]) + dot(x_grp, inv[2 * face : 3 * face, columns])

        def low_part(value, first, column):
            return dot(value, inv[first : first + face, column : column + face])

        low_out[level, 0] = own_part(face)
        low_out[level, 1] = own_part(3 * face)
        lows = [
            send(low_out.at[level, d], low_in.at[level, d], low_send.at[level, d], low_recv.at[level, d], peer)
            for d, peer in enumerate((prev_sub, prev_grp))
        ]
        pending += lows
        if level == 0:
            blocks = [
                send(
                    inv.at[pl.ds(first, face), pl.ds(column, face)], landing.at[d],
                    edge_send.at[i], edge_recv.at[i], peer,
                )
                for i, (first, column, landing, d, peer) in enumerate((
                    (face, face, edge, 0, prev_sub),
                    (3 * face, 3 * face, edge, 1, prev_grp),
                    (3 * face, face, cross, 0, prev_sub),
                    (face, 3 * face, cross, 1, prev_grp),
                ))
            ]
            pending += blocks
            own = rows_c.at[me]
            to_all(lambda peer: send(own, own, rows_send, rows_recv, peer))
            for copy in term_copies:
                copy.wait_recv()
            weight = jnp.concatenate(
                [terms[:, :face] - term_in[0], terms[:, 2 * face : 3 * face] - term_in[1]], axis=1
            )
            weight_high, weight_rest = split(weight)
            load_high[...] = jnp.concatenate([weight_high] * pack, axis=0)
            load_rest[...] = jnp.concatenate([weight_rest] * pack, axis=0)
            part = coarse_part(packed)
        send_coarse(level, part)
        packed, remainder = keep(level, x)
        if level == LEVELS - 1:
            count = LEVELS * right
            first_rows = gram_part(high[:count, :], rest[:count, :])
            for m in range(members):
                part_out[m] = first_rows[m * chunk : (m + 1) * chunk]
            part_near[member] = part_out[member]
            for other, peer in zip(near_others, near_peers):
                send(part_out.at[other], part_near.at[member], part_send.at[0], part_recv.at[0], peer)
        up_sub = own_part(0)
        up_grp = own_part(2 * face)
        for copy in ups:
            copy.wait_recv()
        low_sub, low_grp = up_in[level, 0], up_in[level, 1]
        up_sub = up_sub - low_part(low_sub, face, 0) - low_part(low_grp, 3 * face, 0)
        up_grp = up_grp - low_part(low_sub, face, 2 * face) - low_part(low_grp, 3 * face, 2 * face)
        if level == 0:
            landed(rows_c, devices, rows_send, rows_recv, next_grp)
            raised = exact(rows_c[...].reshape(nco, nco), weight)
            raised_high, raised_rest = split(raised)
            lift_high[...] = jnp.concatenate([raised_high] * pack, axis=0)
            lift_rest[...] = jnp.concatenate([raised_rest] * pack, axis=0)
            for copy in blocks:
                copy.wait_recv()
        up_sub = up_sub + dot(x_sub, edge[0])
        up_grp = up_grp + dot(x_grp, edge[1])
        for copy in diags:
            copy.wait_recv()
        up_sub = up_sub + dot(diag_in[level, 1], cross[0])
        up_grp = up_grp + dot(diag_in[level, 0], cross[1])
        base = jnp.concatenate([up_sub, up_grp], axis=1) - centre * x
        for copy in lows:
            copy.wait_recv()
        base = base - jnp.concatenate([low_in[level, 0], low_in[level, 1]], axis=1)
        landed(direct.at[level], devices, direct_send.at[level], direct_recv.at[level], next_grp)
        image = base + coarse_lift(added(direct.at[level], devices))
        following = image * scale if level == 0 else 2.0 * image * scale - previous
        previous, x = x, following

    packed, remainder = keep(LEVELS, x)
    near[member] = gram_part(packed, remainder)
    broadcast(near, member, near_peers, near_send, near_recv)
    landed(part_near, members, part_send.at[0], part_recv.at[0], near_peers[0])
    part_far[plane] = added(part_near, members)
    broadcast(part_far, plane, far_peers, part_send.at[1], part_recv.at[1])
    landed(near, members, near_send, near_recv, near_peers[0])
    far[plane] = added(near, members)
    broadcast(far, plane, far_peers, far_send, far_recv)
    landed(part_far, planes, part_send.at[1], part_recv.at[1], far_peers[0])
    part_all[member] = added(part_far, planes)
    broadcast(part_all, member, near_peers, part_send.at[2], part_recv.at[2])
    landed(far, planes, far_send, far_recv, far_peers[0])
    last_rows = added(far, planes)
    landed(part_all, members, part_send.at[2], part_recv.at[2], near_peers[0])
    full = jnp.concatenate([part_all[m] for m in range(members)] + [last_rows], axis=0)[:, :order]
    row = lax.broadcasted_iota(jnp.int32, (order, order), 0)
    column = lax.broadcasted_iota(jnp.int32, (order, order), 1)
    below = jnp.where(lax.div(column, right) < lax.div(row, right), full, 0.0)
    same = jnp.where(lax.div(column, right) == lax.div(row, right), full, 0.0)
    gram_ref[...] = (below + same + below.T) * (1.0 / (half * nsub))
    stores.append(pltpu.make_async_copy(gram_ref, gram_hbm, store_sem.at[BLOCKS]))
    stores[-1].start()
    for copy in pending:
        copy.wait_send()
    for copy in stores:
        copy.wait()


def body(nsub, ngrp, residual, bounds, local_inverse, corner_basis, corner_map, coarse_inverse):
    right, half = residual.shape[0], residual.shape[3]
    face = half // 2
    width = 4 * face
    rows, nco = coarse_inverse.shape
    order = BLOCKS * right
    devices = nsub * ngrp
    inner = 1
    while nsub % (2 * inner) == 0 and 2 * inner * ngrp <= nsub // inner:
        inner *= 2
    planes, members = nsub // inner, inner * ngrp
    wide = -(-order // 128) * 128
    pack = 128 // nco if nco < 128 and 128 % nco == 0 and right % (128 // nco) == 0 else 1
    lanes = pack * nco
    chunk = LEVELS * right // members
    hbm = pl.BlockSpec(memory_space=pltpu.HBM)
    dma = pltpu.SemaphoreType.DMA
    f32, bf16 = jnp.float32, jnp.bfloat16
    return pl.pallas_call(
        functools.partial(kernel, nsub, ngrp, inner, pack),
        out_shape=(
            jax.ShapeDtypeStruct((BLOCKS, right, 1, 1, half), f32),
            jax.ShapeDtypeStruct((order, order), f32),
        ),
        in_specs=[hbm] * 6,
        out_specs=(hbm, hbm),
        scratch_shapes=[
            pltpu.VMEM((BLOCKS, right, 1, 1, half), f32),
            pltpu.VMEM((order, order), f32),
            pltpu.SMEM(bounds.shape, f32),
            pltpu.VMEM(residual.shape, f32),
            pltpu.VMEM((width, width), bf16),
            pltpu.VMEM(corner_basis.shape, bf16),
            pltpu.VMEM(corner_map.shape, corner_map.dtype),
            pltpu.VMEM((LEVELS, 2, right, face), bf16),
            pltpu.VMEM((LEVELS, 2, right, face), bf16),
            pltpu.VMEM((LEVELS, 2, right, face), bf16),
            pltpu.VMEM((LEVELS, 2, right, face), f32),
            pltpu.VMEM((LEVELS, 2, right, face), f32),
            pltpu.VMEM((2, nco, face), f32),
            pltpu.VMEM((2, nco, face), f32),
            pltpu.VMEM((2, face, face), bf16),
            pltpu.VMEM((2, face, face), bf16),
            pltpu.VMEM((devices, rows, nco), f32),
            pltpu.VMEM((LEVELS, devices, right // pack, lanes), f32),
            pltpu.VMEM((members, chunk, wide), f32),
            pltpu.VMEM((members, chunk, wide), f32),
            pltpu.VMEM((planes, chunk, wide), f32),
            pltpu.VMEM((members, chunk, wide), f32),
            pltpu.VMEM((members, right, wide), f32),
            pltpu.VMEM((planes, right, wide), f32),
            pltpu.VMEM((wide, half), bf16),
            pltpu.VMEM((wide, half), bf16),
            pltpu.VMEM((lanes, half), bf16),
            pltpu.VMEM((lanes, half), bf16),
            pltpu.VMEM((lanes, half), bf16),
            pltpu.VMEM((lanes, half), bf16),
            dma((6,)),
            dma((BLOCKS + 1,)),
            dma((LEVELS, 2)),
            dma((LEVELS, 2)),
            dma((LEVELS, 2)),
            dma((LEVELS, 2)),
            dma((LEVELS, 2)),
            dma((LEVELS, 2)),
            dma((2,)),
            dma((2,)),
            dma((4,)),
            dma((4,)),
            dma,
            dma,
            dma((LEVELS,)),
            dma((LEVELS,)),
            dma((3,)),
            dma((3,)),
            dma,
            dma,
            dma,
            dma,
        ],
        compiler_params=pltpu.CompilerParams(
            collective_id=0, has_side_effects=True, vmem_limit_bytes=60 * 1024 * 1024
        ),
    )(bounds, residual, local_inverse, corner_basis, corner_map, coarse_inverse)


def solution(mesh):
    in_specs = (
        P(None, "sub", "grp", None),
        P(),
        P("sub", "grp", None, None),
        P("sub", "grp", None, None),
        P("sub", "grp", None),
        P(("sub", "grp"), None),
    )
    out_specs = (P(None, None, "sub", "grp", None), P())
    run = functools.partial(body, mesh.shape["sub"], mesh.shape["grp"])
    return jax.shard_map(run, mesh=mesh, in_specs=in_specs, out_specs=out_specs, check_vma=False)
```

```python
import functools

import jax
import jax.numpy as jnp
from jax import lax
from jax.experimental import pallas as pl
from jax.experimental.pallas import tpu as pltpu
from jax.sharding import PartitionSpec as P

S_STEP = 2
BLOCKS = 2 * S_STEP + 1
LEVELS = 2 * S_STEP
LOGICAL = pl.DeviceIdType.LOGICAL
HIGHEST = lax.Precision.HIGHEST


def exact(a, b):
    return jnp.dot(a, b, precision=HIGHEST, preferred_element_type=jnp.float32)


def across_rows(a, b, precision=None):
    return lax.dot_general(
        a, b, (((1,), (1,)), ((), ())), precision=precision, preferred_element_type=jnp.float32
    )


def dot(a, b):
    return jnp.dot(a, b, preferred_element_type=jnp.float32)


def kernel(
    nsub, ngrp, inner, pack,
    bounds_hbm, res_hbm, inv_hbm, corner_hbm, map_hbm, coarse_hbm,
    basis_hbm, gram_hbm,
    basis_ref, gram_ref, bounds, res, inv, corner, ids_ref,
    up_out, up_in, diag_in, low_out, low_in, term_out, term_in, edge, cross,
    rows_c, direct, part_out, part_near, part_far, part_all, near, far,
    high, rest, load_high, load_rest, lift_high, lift_rest,
    load_sem, store_sem, up_send, up_recv, diag_send, diag_recv, low_send, low_recv,
    term_send, term_recv, edge_send, edge_recv, rows_send, rows_recv, direct_send, direct_recv,
    part_send, part_recv, near_send, near_recv, far_send, far_recv,
):
    right, half = up_out.shape[2], high.shape[1]
    face = half // 2
    order = BLOCKS * right
    nco = rows_c.shape[2]
    planes = nsub // inner
    members = inner * ngrp
    devices = nsub * ngrp
    packed_rows = right // pack
    chunk = part_out.shape[1]
    sub = lax.axis_index("sub")
    grp = lax.axis_index("grp")
    me = sub * ngrp + grp
    plane = lax.div(sub, inner)
    within = lax.rem(sub, inner)
    member = within * ngrp + grp
    sub_up, sub_down = lax.rem(sub + 1, nsub), lax.rem(sub + nsub - 1, nsub)
    grp_up, grp_down = lax.rem(grp + 1, ngrp), lax.rem(grp + ngrp - 1, ngrp)
    next_sub, prev_sub = sub_up * ngrp + grp, sub_down * ngrp + grp
    next_grp, prev_grp = sub * ngrp + grp_up, sub * ngrp + grp_down
    diagonal_peers = (sub_up * ngrp + grp_down, sub_down * ngrp + grp_up)

    def to_all(action):
        def step(offset, carry):
            other = me + offset
            action(jnp.where(other >= devices, other - devices, other))
            return carry

        lax.fori_loop(1, devices, step, 0, unroll=devices <= 64)

    near_others = [lax.rem(member + o, members) for o in range(1, members)]
    near_peers = [plane * members + o for o in near_others]
    far_peers = [lax.rem(plane + o, planes) * members + member for o in range(1, planes)]

    barrier = pltpu.get_barrier_semaphore()
    loads = [
        pltpu.make_async_copy(src, dst, load_sem.at[i])
        for i, (src, dst) in enumerate((
            (corner_hbm, corner),
            (map_hbm, ids_ref),
            (res_hbm, res),
            (coarse_hbm, rows_c.at[me]),
            (bounds_hbm, bounds),
            (inv_hbm.at[0, 0], inv),
        ))
    ]
    for copy in loads:
        copy.start()
    to_all(lambda peer: pl.semaphore_signal(barrier, inc=1, device_id=peer, device_id_type=LOGICAL))

    def send(src, dst, send_sem, recv_sem, peer):
        copy = pltpu.make_async_remote_copy(
            src_ref=src, dst_ref=dst, send_sem=send_sem, recv_sem=recv_sem,
            device_id=peer, device_id_type=LOGICAL,
        )
        copy.start()
        return copy

    pending = []
    stores = []

    def landed(buf, count, send_sem, recv_sem, peer):
        part = buf.at[pl.ds(0, count - 1)]
        copy = pltpu.make_async_remote_copy(
            src_ref=part, dst_ref=part, send_sem=send_sem, recv_sem=recv_sem,
            device_id=peer, device_id_type=LOGICAL,
        )
        copy.wait_recv()
        pending.append(copy)

    def split(value):
        rough = value.astype(jnp.bfloat16)
        return rough, (value - rough.astype(jnp.float32)).astype(jnp.bfloat16)

    def added(buf, count):
        total = buf[0]
        for i in range(1, count):
            total = total + buf[i]
        return total

    def broadcast(buf, slot, peers, send_sem, recv_sem):
        own = buf.at[slot]
        for peer in peers:
            send(own, own, send_sem, recv_sem, peer)

    high[...] = jnp.zeros_like(high)
    rest[...] = jnp.zeros_like(rest)
    loads[0].wait()
    loads[1].wait()
    ids = ids_ref[0]
    table = (lax.broadcasted_iota(jnp.int32, (nco, ids.shape[1]), 0) == ids).astype(jnp.bfloat16)
    terms = dot(table, corner[0, 0])
    term_out[0] = terms[:, face : 2 * face]
    term_out[1] = terms[:, 3 * face :]
    for copy in loads[2:5]:
        copy.wait()
    x = res[:, 0, 0, :]
    centre = (bounds[0] + bounds[1]) / 2.0
    radius = (bounds[1] - bounds[0]) / 2.0
    scale = 1.0 / jnp.full((right, half), radius, jnp.float32)
    lane = lax.broadcasted_iota(jnp.int32, (right, pack * nco), 1)
    row = lax.broadcasted_iota(jnp.int32, (right, pack * nco), 0)
    mine = lax.div(lane, nco) == lax.div(row, packed_rows)

    def gram_part(first, second):
        both = across_rows(jnp.concatenate([first, second], axis=0), high[...])
        count = first.shape[0]
        return both[:count] + (both[count:] + across_rows(first, rest[...]))

    def coarse_part(packed):
        part = across_rows(packed, load_high[...]) + across_rows(packed, load_rest[...])
        if pack == 1:
            return part
        part = jnp.where(mine, part, 0.0)
        total = part[:packed_rows]
        for q in range(1, pack):
            total = total + part[q * packed_rows : (q + 1) * packed_rows]
        return total

    def coarse_lift(total):
        if pack > 1:
            total = jnp.where(mine, jnp.concatenate([total] * pack, axis=0), 0.0)
        total_high, total_rest = split(total)
        both = dot(jnp.concatenate([total_high, total_rest], axis=0), lift_high[...])
        return both[:right] + (both[right:] + dot(total_high, lift_rest[...]))

    def send_coarse(level, part):
        direct[level, me] = part
        own = direct.at[level, me]
        to_all(lambda peer: send(own, own, direct_send.at[level], direct_recv.at[level], peer))

    def keep(level, value):
        packed, remainder = split(value)
        basis_ref[level, :, 0, 0, :] = value
        high[pl.ds(level * right, right), :] = packed
        rest[pl.ds(level * right, right), :] = remainder
        stores.append(pltpu.make_async_copy(basis_ref.at[level], basis_hbm.at[level], store_sem.at[level]))
        stores[-1].start()
        return packed, remainder

    pl.semaphore_wait(barrier, devices - 1)
    term_copies = [
        send(term_out.at[d], term_in.at[d], term_send.at[d], term_recv.at[d], peer)
        for d, peer in enumerate((prev_sub, prev_grp))
    ]
    pending += term_copies

    previous = None
    for level in range(LEVELS):
        packed = x.astype(jnp.bfloat16)
        x_sub, x_grp = packed[:, :face], packed[:, face:]
        up_out[level, 0] = x_sub
        up_out[level, 1] = x_grp
        ups = [
            send(up_out.at[level, d], up_in.at[level, d], up_send.at[level, d], up_recv.at[level, d], peer)
            for d, peer in enumerate((next_sub, next_grp))
        ]
        diags = [
            send(up_out.at[level, d], diag_in.at[level, d], diag_send.at[level, d], diag_recv.at[level, d], peer)
            for d, peer in enumerate(diagonal_peers)
        ] if level > 0 else []
        pending += ups + diags
        if level > 0:
            part = coarse_part(packed)
        else:
            loads[5].wait()
            blocks = [
                send(
                    inv.at[pl.ds(first, face), pl.ds(column, face)], landing.at[d],
                    edge_send.at[i], edge_recv.at[i], peer,
                )
                for i, (first, column, landing, d, peer) in enumerate((
                    (face, face, edge, 0, prev_sub),
                    (3 * face, face, cross, 0, prev_sub),
                    (3 * face, 3 * face, edge, 1, prev_grp),
                    (face, 3 * face, cross, 1, prev_grp),
                ))
            ]
            pending += blocks
            own = rows_c.at[me]
            to_all(lambda peer: send(own, own, rows_send, rows_recv, peer))

        def own_part(first):
            columns = slice(first, first + face)
            return dot(x_sub, inv[:face, columns]) + dot(x_grp, inv[2 * face : 3 * face, columns])

        def low_part(value, first, column):
            return dot(value, inv[first : first + face, column : column + face])

        def send_lows(first, second):
            low_out[level, 0] = first
            low_out[level, 1] = second
            copies = [
                send(low_out.at[level, d], low_in.at[level, d], low_send.at[level, d], low_recv.at[level, d], peer)
                for d, peer in enumerate((prev_sub, prev_grp))
            ]
            pending.extend(copies)
            return copies

        first_low, second_low = own_part(face), own_part(3 * face)
        if level > 0:
            lows = send_lows(first_low, second_low)
        else:
            for copy in ups:
                copy.wait_recv()
            low_sub, low_grp = up_in[level, 0], up_in[level, 1]
            lows = send_lows(
                first_low - low_part(low_sub, face, face) - low_part(low_grp, 3 * face, face),
                second_low - low_part(low_sub, face, 3 * face) - low_part(low_grp, 3 * face, 3 * face),
            )
            for copy in term_copies:
                copy.wait_recv()
            weight = jnp.concatenate(
                [terms[:, :face] - term_in[0], terms[:, 2 * face : 3 * face] - term_in[1]], axis=1
            )
            weight_high, weight_rest = split(weight)
            load_high[...] = jnp.concatenate([weight_high] * pack, axis=0)
            load_rest[...] = jnp.concatenate([weight_rest] * pack, axis=0)
            part = coarse_part(packed)
        send_coarse(level, part)
        packed, remainder = keep(level, x)
        if level == LEVELS - 1:
            count = LEVELS * right
            first_rows = gram_part(high[:count, :], rest[:count, :])
            for m in range(members):
                part_out[m] = first_rows[m * chunk : (m + 1) * chunk]
            part_near[member] = part_out[member]
            for other, peer in zip(near_others, near_peers):
                send(part_out.at[other], part_near.at[member], part_send.at[0], part_recv.at[0], peer)
        up_sub = own_part(0)
        up_grp = own_part(2 * face)
        if level > 0:
            for copy in ups:
                copy.wait_recv()
            low_sub, low_grp = up_in[level, 0], up_in[level, 1]
        up_sub = up_sub - low_part(low_sub, face, 0) - low_part(low_grp, 3 * face, 0)
        up_grp = up_grp - low_part(low_sub, face, 2 * face) - low_part(low_grp, 3 * face, 2 * face)
        if level == 0:
            landed(rows_c, devices, rows_send, rows_recv, next_grp)
            raised = exact(rows_c[...].reshape(nco, nco), weight)
            raised_high, raised_rest = split(raised)
            lift_high[...] = jnp.concatenate([raised_high] * pack, axis=0)
            lift_rest[...] = jnp.concatenate([raised_rest] * pack, axis=0)
        else:
            if level == 1:
                for copy in blocks:
                    copy.wait_recv()
            up_sub = up_sub + dot(x_sub, edge[0])
            up_grp = up_grp + dot(x_grp, edge[1])
            for copy in diags:
                copy.wait_recv()
            up_sub = up_sub + dot(diag_in[level, 1], cross[0])
            up_grp = up_grp + dot(diag_in[level, 0], cross[1])
        base = jnp.concatenate([up_sub, up_grp], axis=1) - centre * x
        for copy in lows:
            copy.wait_recv()
        base = base - jnp.concatenate([low_in[level, 0], low_in[level, 1]], axis=1)
        landed(direct.at[level], devices, direct_send.at[level], direct_recv.at[level], next_grp)
        image = base + coarse_lift(added(direct.at[level], devices))
        following = image * scale if level == 0 else 2.0 * image * scale - previous
        previous, x = x, following

    packed, remainder = keep(LEVELS, x)
    near[member] = gram_part(packed, remainder)
    broadcast(near, member, near_peers, near_send, near_recv)
    landed(part_near, members, part_send.at[0], part_recv.at[0], near_peers[0])
    part_far[plane] = added(part_near, members)
    broadcast(part_far, plane, far_peers, part_send.at[1], part_recv.at[1])
    landed(near, members, near_send, near_recv, near_peers[0])
    far[plane] = added(near, members)
    broadcast(far, plane, far_peers, far_send, far_recv)
    landed(part_far, planes, part_send.at[1], part_recv.at[1], far_peers[0])
    part_all[member] = added(part_far, planes)
    broadcast(part_all, member, near_peers, part_send.at[2], part_recv.at[2])
    landed(far, planes, far_send, far_recv, far_peers[0])
    last_rows = added(far, planes)
    landed(part_all, members, part_send.at[2], part_recv.at[2], near_peers[0])
    full = jnp.concatenate([part_all[m] for m in range(members)] + [last_rows], axis=0)[:, :order]
    row = lax.broadcasted_iota(jnp.int32, (order, order), 0)
    column = lax.broadcasted_iota(jnp.int32, (order, order), 1)
    below = jnp.where(lax.div(column, right) < lax.div(row, right), full, 0.0)
    same = jnp.where(lax.div(column, right) == lax.div(row, right), full, 0.0)
    gram_ref[...] = (below + same + below.T) * (1.0 / (half * nsub))
    stores.append(pltpu.make_async_copy(gram_ref, gram_hbm, store_sem.at[BLOCKS]))
    stores[-1].start()
    for copy in pending:
        copy.wait_send()
    for copy in stores:
        copy.wait()


def body(nsub, ngrp, residual, bounds, local_inverse, corner_basis, corner_map, coarse_inverse):
    right, half = residual.shape[0], residual.shape[3]
    face = half // 2
    width = 4 * face
    rows, nco = coarse_inverse.shape
    order = BLOCKS * right
    devices = nsub * ngrp
    inner = 1
    while nsub % (2 * inner) == 0 and 2 * inner * ngrp <= nsub // inner:
        inner *= 2
    planes, members = nsub // inner, inner * ngrp
    wide = -(-order // 128) * 128
    pack = 128 // nco if nco < 128 and 128 % nco == 0 and right % (128 // nco) == 0 else 1
    lanes = pack * nco
    chunk = LEVELS * right // members
    hbm = pl.BlockSpec(memory_space=pltpu.HBM)
    dma = pltpu.SemaphoreType.DMA
    f32, bf16 = jnp.float32, jnp.bfloat16
    return pl.pallas_call(
        functools.partial(kernel, nsub, ngrp, inner, pack),
        out_shape=(
            jax.ShapeDtypeStruct((BLOCKS, right, 1, 1, half), f32),
            jax.ShapeDtypeStruct((order, order), f32),
        ),
        in_specs=[hbm] * 6,
        out_specs=(hbm, hbm),
        scratch_shapes=[
            pltpu.VMEM((BLOCKS, right, 1, 1, half), f32),
            pltpu.VMEM((order, order), f32),
            pltpu.SMEM(bounds.shape, f32),
            pltpu.VMEM(residual.shape, f32),
            pltpu.VMEM((width, width), bf16),
            pltpu.VMEM(corner_basis.shape, bf16),
            pltpu.VMEM(corner_map.shape, corner_map.dtype),
            pltpu.VMEM((LEVELS, 2, right, face), bf16),
            pltpu.VMEM((LEVELS, 2, right, face), bf16),
            pltpu.VMEM((LEVELS, 2, right, face), bf16),
            pltpu.VMEM((LEVELS, 2, right, face), f32),
            pltpu.VMEM((LEVELS, 2, right, face), f32),
            pltpu.VMEM((2, nco, face), f32),
            pltpu.VMEM((2, nco, face), f32),
            pltpu.VMEM((2, face, face), bf16),
            pltpu.VMEM((2, face, face), bf16),
            pltpu.VMEM((devices, rows, nco), f32),
            pltpu.VMEM((LEVELS, devices, right // pack, lanes), f32),
            pltpu.VMEM((members, chunk, wide), f32),
            pltpu.VMEM((members, chunk, wide), f32),
            pltpu.VMEM((planes, chunk, wide), f32),
            pltpu.VMEM((members, chunk, wide), f32),
            pltpu.VMEM((members, right, wide), f32),
            pltpu.VMEM((planes, right, wide), f32),
            pltpu.VMEM((wide, half), bf16),
            pltpu.VMEM((wide, half), bf16),
            pltpu.VMEM((lanes, half), bf16),
            pltpu.VMEM((lanes, half), bf16),
            pltpu.VMEM((lanes, half), bf16),
            pltpu.VMEM((lanes, half), bf16),
            dma((6,)),
            dma((BLOCKS + 1,)),
            dma((LEVELS, 2)),
            dma((LEVELS, 2)),
            dma((LEVELS, 2)),
            dma((LEVELS, 2)),
            dma((LEVELS, 2)),
            dma((LEVELS, 2)),
            dma((2,)),
            dma((2,)),
            dma((4,)),
            dma((4,)),
            dma,
            dma,
            dma((LEVELS,)),
            dma((LEVELS,)),
            dma((3,)),
            dma((3,)),
            dma,
            dma,
            dma,
            dma,
        ],
        compiler_params=pltpu.CompilerParams(
            collective_id=0, has_side_effects=True, vmem_limit_bytes=60 * 1024 * 1024
        ),
    )(bounds, residual, local_inverse, corner_basis, corner_map, coarse_inverse)


def solution(mesh):
    in_specs = (
        P(None, "sub", "grp", None),
        P(),
        P("sub", "grp", None, None),
        P("sub", "grp", None, None),
        P("sub", "grp", None),
        P(("sub", "grp"), None),
    )
    out_specs = (P(None, None, "sub", "grp", None), P())
    run = functools.partial(body, mesh.shape["sub"], mesh.shape["grp"])
    return jax.shard_map(run, mesh=mesh, in_specs=in_specs, out_specs=out_specs, check_vma=False)
```

```python
import functools

import jax
import jax.numpy as jnp
from jax import lax
from jax.experimental import pallas as pl
from jax.experimental.pallas import tpu as pltpu
from jax.sharding import PartitionSpec as P

S_STEP = 2
BLOCKS = 2 * S_STEP + 1
LEVELS = 2 * S_STEP
LOGICAL = pl.DeviceIdType.LOGICAL
HIGHEST = lax.Precision.HIGHEST


def exact(a, b):
    return jnp.dot(a, b, precision=HIGHEST, preferred_element_type=jnp.float32)


def across_rows(a, b, precision=None):
    return lax.dot_general(
        a, b, (((1,), (1,)), ((), ())), precision=precision, preferred_element_type=jnp.float32
    )


def dot(a, b):
    return jnp.dot(a, b, preferred_element_type=jnp.float32)


def kernel(
    nsub, ngrp, inner, pack,
    bounds_hbm, res_hbm, inv_hbm, corner_hbm, map_hbm, coarse_hbm,
    basis_hbm, gram_hbm,
    basis_ref, gram_ref, bounds, res, inv, corner, ids_ref,
    up_out, up_in, diag_in, low_out, low_in, term_out, term_in, edge, cross,
    rows_c, direct, part_out, part_near, part_far, part_all, near, far,
    high, rest, load_high, load_rest, lift_high, lift_rest,
    load_sem, store_sem, up_send, up_recv, diag_send, diag_recv, low_send, low_recv,
    term_send, term_recv, edge_send, edge_recv, rows_send, rows_recv, direct_send, direct_recv,
    part_send, part_recv, near_send, near_recv, far_send, far_recv,
):
    right, half = up_out.shape[2], high.shape[1]
    face = half // 2
    order = BLOCKS * right
    nco = rows_c.shape[2]
    planes = nsub // inner
    members = inner * ngrp
    devices = nsub * ngrp
    packed_rows = right // pack
    chunk = part_out.shape[1]
    sub = lax.axis_index("sub")
    grp = lax.axis_index("grp")
    me = sub * ngrp + grp
    plane = lax.div(sub, inner)
    within = lax.rem(sub, inner)
    member = within * ngrp + grp
    sub_up, sub_down = lax.rem(sub + 1, nsub), lax.rem(sub + nsub - 1, nsub)
    grp_up, grp_down = lax.rem(grp + 1, ngrp), lax.rem(grp + ngrp - 1, ngrp)
    next_sub, prev_sub = sub_up * ngrp + grp, sub_down * ngrp + grp
    next_grp, prev_grp = sub * ngrp + grp_up, sub * ngrp + grp_down
    diagonal_peers = (sub_up * ngrp + grp_down, sub_down * ngrp + grp_up)

    def to_all(action):
        def step(offset, carry):
            other = me + offset
            action(jnp.where(other >= devices, other - devices, other))
            return carry

        lax.fori_loop(1, devices, step, 0, unroll=devices <= 64)

    near_others = [lax.rem(member + o, members) for o in range(1, members)]
    near_peers = [plane * members + o for o in near_others]
    far_peers = [lax.rem(plane + o, planes) * members + member for o in range(1, planes)]

    barrier = pltpu.get_barrier_semaphore()
    loads = [
        pltpu.make_async_copy(src, dst, load_sem.at[i])
        for i, (src, dst) in enumerate((
            (corner_hbm, corner),
            (map_hbm, ids_ref),
            (res_hbm, res),
            (coarse_hbm, rows_c.at[me]),
            (bounds_hbm, bounds),
            (inv_hbm.at[0, 0], inv),
        ))
    ]
    for copy in loads:
        copy.start()
    to_all(lambda peer: pl.semaphore_signal(barrier, inc=1, device_id=peer, device_id_type=LOGICAL))

    def send(src, dst, send_sem, recv_sem, peer):
        copy = pltpu.make_async_remote_copy(
            src_ref=src, dst_ref=dst, send_sem=send_sem, recv_sem=recv_sem,
            device_id=peer, device_id_type=LOGICAL,
        )
        copy.start()
        return copy

    pending = []
    stores = []

    def landed(buf, count, send_sem, recv_sem, peer):
        part = buf.at[pl.ds(0, count - 1)]
        copy = pltpu.make_async_remote_copy(
            src_ref=part, dst_ref=part, send_sem=send_sem, recv_sem=recv_sem,
            device_id=peer, device_id_type=LOGICAL,
        )
        copy.wait_recv()
        pending.append(copy)

    def split(value):
        rough = value.astype(jnp.bfloat16)
        return rough, (value - rough.astype(jnp.float32)).astype(jnp.bfloat16)

    def added(buf, count):
        total = buf[0]
        for i in range(1, count):
            total = total + buf[i]
        return total

    def broadcast(buf, slot, peers, send_sem, recv_sem):
        own = buf.at[slot]
        for peer in peers:
            send(own, own, send_sem, recv_sem, peer)

    def send_blocks(place, landing, corners_of):
        copies = [
            send(
                inv.at[pl.ds(first, face), pl.ds(column, face)], landing.at[d],
                edge_send.at[place + d], edge_recv.at[place + d], peer,
            )
            for d, ((first, column), peer) in enumerate(zip(corners_of, (prev_sub, prev_grp)))
        ]
        pending.extend(copies)
        return copies

    high[...] = jnp.zeros_like(high)
    rest[...] = jnp.zeros_like(rest)
    loads[0].wait()
    loads[1].wait()
    ids = ids_ref[0]
    table = (lax.broadcasted_iota(jnp.int32, (nco, ids.shape[1]), 0) == ids).astype(jnp.bfloat16)
    terms = dot(table, corner[0, 0])
    term_out[0] = terms[:, face : 2 * face]
    term_out[1] = terms[:, 3 * face :]
    for copy in loads[2:5]:
        copy.wait()
    x = res[:, 0, 0, :]
    centre = (bounds[0] + bounds[1]) / 2.0
    radius = (bounds[1] - bounds[0]) / 2.0
    scale = 1.0 / jnp.full((right, half), radius, jnp.float32)
    lane = lax.broadcasted_iota(jnp.int32, (right, pack * nco), 1)
    row = lax.broadcasted_iota(jnp.int32, (right, pack * nco), 0)
    mine = lax.div(lane, nco) == lax.div(row, packed_rows)

    def gram_part(first, second):
        both = across_rows(jnp.concatenate([first, second], axis=0), high[...])
        count = first.shape[0]
        return both[:count] + (both[count:] + across_rows(first, rest[...]))

    def coarse_part(packed):
        part = across_rows(packed, load_high[...]) + across_rows(packed, load_rest[...])
        if pack == 1:
            return part
        part = jnp.where(mine, part, 0.0)
        total = part[:packed_rows]
        for q in range(1, pack):
            total = total + part[q * packed_rows : (q + 1) * packed_rows]
        return total

    def coarse_lift(total):
        if pack > 1:
            total = jnp.where(mine, jnp.concatenate([total] * pack, axis=0), 0.0)
        total_high, total_rest = split(total)
        both = dot(jnp.concatenate([total_high, total_rest], axis=0), lift_high[...])
        return both[:right] + (both[right:] + dot(total_high, lift_rest[...]))

    def send_coarse(level, part):
        direct[level, me] = part
        own = direct.at[level, me]
        to_all(lambda peer: send(own, own, direct_send.at[level], direct_recv.at[level], peer))

    def keep(level, value):
        packed, remainder = split(value)
        basis_ref[level, :, 0, 0, :] = value
        high[pl.ds(level * right, right), :] = packed
        rest[pl.ds(level * right, right), :] = remainder
        stores.append(pltpu.make_async_copy(basis_ref.at[level], basis_hbm.at[level], store_sem.at[level]))
        stores[-1].start()
        return packed, remainder

    pl.semaphore_wait(barrier, devices - 1)
    term_copies = [
        send(term_out.at[d], term_in.at[d], term_send.at[d], term_recv.at[d], peer)
        for d, peer in enumerate((prev_sub, prev_grp))
    ]
    pending += term_copies

    previous = None
    for level in range(LEVELS):
        packed = x.astype(jnp.bfloat16)
        x_sub, x_grp = packed[:, :face], packed[:, face:]
        up_out[level, 0] = x_sub
        up_out[level, 1] = x_grp
        ups = [
            send(up_out.at[level, d], up_in.at[level, d], up_send.at[level, d], up_recv.at[level, d], peer)
            for d, peer in enumerate((next_sub, next_grp))
        ]
        diags = [
            send(up_out.at[level, d], diag_in.at[level, d], diag_send.at[level, d], diag_recv.at[level, d], peer)
            for d, peer in enumerate(diagonal_peers)
        ] if level > 0 else []
        pending += ups + diags
        if level > 0:
            part = coarse_part(packed)
        else:
            own = rows_c.at[me]
            to_all(lambda peer: send(own, own, rows_send, rows_recv, peer))
            loads[5].wait()
            blocks = send_blocks(0, edge, ((face, face), (3 * face, 3 * face)))

        def own_part(first):
            columns = slice(first, first + face)
            return dot(x_sub, inv[:face, columns]) + dot(x_grp, inv[2 * face : 3 * face, columns])

        def low_part(value, first, column):
            return dot(value, inv[first : first + face, column : column + face])

        def send_lows(first, second):
            low_out[level, 0] = first
            low_out[level, 1] = second
            copies = [
                send(low_out.at[level, d], low_in.at[level, d], low_send.at[level, d], low_recv.at[level, d], peer)
                for d, peer in enumerate((prev_sub, prev_grp))
            ]
            pending.extend(copies)
            return copies

        first_low, second_low = own_part(face), own_part(3 * face)
        if level > 0:
            lows = send_lows(first_low, second_low)
        else:
            for copy in term_copies:
                copy.wait_recv()
            weight = jnp.concatenate(
                [terms[:, :face] - term_in[0], terms[:, 2 * face : 3 * face] - term_in[1]], axis=1
            )
            weight_high, weight_rest = split(weight)
            load_high[...] = jnp.concatenate([weight_high] * pack, axis=0)
            load_rest[...] = jnp.concatenate([weight_rest] * pack, axis=0)
            part = coarse_part(packed)
        send_coarse(level, part)
        if level == 0:
            for copy in ups:
                copy.wait_recv()
            low_sub, low_grp = up_in[level, 0], up_in[level, 1]
            lows = send_lows(
                first_low - low_part(low_sub, face, face) - low_part(low_grp, 3 * face, face),
                second_low - low_part(low_sub, face, 3 * face) - low_part(low_grp, 3 * face, 3 * face),
            )
            blocks += send_blocks(2, cross, ((3 * face, face), (face, 3 * face)))
        packed, remainder = keep(level, x)
        if level == LEVELS - 1:
            count = LEVELS * right
            first_rows = gram_part(high[:count, :], rest[:count, :])
            for m in range(members):
                part_out[m] = first_rows[m * chunk : (m + 1) * chunk]
            part_near[member] = part_out[member]
            for other, peer in zip(near_others, near_peers):
                send(part_out.at[other], part_near.at[member], part_send.at[0], part_recv.at[0], peer)
        up_sub = own_part(0)
        up_grp = own_part(2 * face)
        if level > 0:
            for copy in ups:
                copy.wait_recv()
            low_sub, low_grp = up_in[level, 0], up_in[level, 1]
        up_sub = up_sub - low_part(low_sub, face, 0) - low_part(low_grp, 3 * face, 0)
        up_grp = up_grp - low_part(low_sub, face, 2 * face) - low_part(low_grp, 3 * face, 2 * face)
        if level == 0:
            landed(rows_c, devices, rows_send, rows_recv, next_grp)
            raised = exact(rows_c[...].reshape(nco, nco), weight)
            raised_high, raised_rest = split(raised)
            lift_high[...] = jnp.concatenate([raised_high] * pack, axis=0)
            lift_rest[...] = jnp.concatenate([raised_rest] * pack, axis=0)
        else:
            if level == 1:
                for copy in blocks:
                    copy.wait_recv()
            up_sub = up_sub + dot(x_sub, edge[0])
            up_grp = up_grp + dot(x_grp, edge[1])
            for copy in diags:
                copy.wait_recv()
            up_sub = up_sub + dot(diag_in[level, 1], cross[0])
            up_grp = up_grp + dot(diag_in[level, 0], cross[1])
        base = jnp.concatenate([up_sub, up_grp], axis=1) - centre * x
        for copy in lows:
            copy.wait_recv()
        base = base - jnp.concatenate([low_in[level, 0], low_in[level, 1]], axis=1)
        landed(direct.at[level], devices, direct_send.at[level], direct_recv.at[level], next_grp)
        image = base + coarse_lift(added(direct.at[level], devices))
        following = image * scale if level == 0 else 2.0 * image * scale - previous
        previous, x = x, following

    packed, remainder = keep(LEVELS, x)
    near[member] = gram_part(packed, remainder)
    broadcast(near, member, near_peers, near_send, near_recv)
    landed(part_near, members, part_send.at[0], part_recv.at[0], near_peers[0])
    part_far[plane] = added(part_near, members)
    broadcast(part_far, plane, far_peers, part_send.at[1], part_recv.at[1])
    landed(near, members, near_send, near_recv, near_peers[0])
    far[plane] = added(near, members)
    broadcast(far, plane, far_peers, far_send, far_recv)
    landed(part_far, planes, part_send.at[1], part_recv.at[1], far_peers[0])
    part_all[member] = added(part_far, planes)
    broadcast(part_all, member, near_peers, part_send.at[2], part_recv.at[2])
    landed(far, planes, far_send, far_recv, far_peers[0])
    last_rows = added(far, planes)
    landed(part_all, members, part_send.at[2], part_recv.at[2], near_peers[0])
    full = jnp.concatenate([part_all[m] for m in range(members)] + [last_rows], axis=0)[:, :order]
    row = lax.broadcasted_iota(jnp.int32, (order, order), 0)
    column = lax.broadcasted_iota(jnp.int32, (order, order), 1)
    below = jnp.where(lax.div(column, right) < lax.div(row, right), full, 0.0)
    same = jnp.where(lax.div(column, right) == lax.div(row, right), full, 0.0)
    gram_ref[...] = (below + same + below.T) * (1.0 / (half * nsub))
    stores.append(pltpu.make_async_copy(gram_ref, gram_hbm, store_sem.at[BLOCKS]))
    stores[-1].start()
    for copy in pending:
        copy.wait_send()
    for copy in stores:
        copy.wait()


def body(nsub, ngrp, residual, bounds, local_inverse, corner_basis, corner_map, coarse_inverse):
    right, half = residual.shape[0], residual.shape[3]
    face = half // 2
    width = 4 * face
    rows, nco = coarse_inverse.shape
    order = BLOCKS * right
    devices = nsub * ngrp
    inner = 1
    while nsub % (2 * inner) == 0 and 2 * inner * ngrp <= nsub // inner:
        inner *= 2
    planes, members = nsub // inner, inner * ngrp
    wide = -(-order // 128) * 128
    pack = 128 // nco if nco < 128 and 128 % nco == 0 and right % (128 // nco) == 0 else 1
    lanes = pack * nco
    chunk = LEVELS * right // members
    hbm = pl.BlockSpec(memory_space=pltpu.HBM)
    dma = pltpu.SemaphoreType.DMA
    f32, bf16 = jnp.float32, jnp.bfloat16
    return pl.pallas_call(
        functools.partial(kernel, nsub, ngrp, inner, pack),
        out_shape=(
            jax.ShapeDtypeStruct((BLOCKS, right, 1, 1, half), f32),
            jax.ShapeDtypeStruct((order, order), f32),
        ),
        in_specs=[hbm] * 6,
        out_specs=(hbm, hbm),
        scratch_shapes=[
            pltpu.VMEM((BLOCKS, right, 1, 1, half), f32),
            pltpu.VMEM((order, order), f32),
            pltpu.SMEM(bounds.shape, f32),
            pltpu.VMEM(residual.shape, f32),
            pltpu.VMEM((width, width), bf16),
            pltpu.VMEM(corner_basis.shape, bf16),
            pltpu.VMEM(corner_map.shape, corner_map.dtype),
            pltpu.VMEM((LEVELS, 2, right, face), bf16),
            pltpu.VMEM((LEVELS, 2, right, face), bf16),
            pltpu.VMEM((LEVELS, 2, right, face), bf16),
            pltpu.VMEM((LEVELS, 2, right, face), f32),
            pltpu.VMEM((LEVELS, 2, right, face), f32),
            pltpu.VMEM((2, nco, face), f32),
            pltpu.VMEM((2, nco, face), f32),
            pltpu.VMEM((2, face, face), bf16),
            pltpu.VMEM((2, face, face), bf16),
            pltpu.VMEM((devices, rows, nco), f32),
            pltpu.VMEM((LEVELS, devices, right // pack, lanes), f32),
            pltpu.VMEM((members, chunk, wide), f32),
            pltpu.VMEM((members, chunk, wide), f32),
            pltpu.VMEM((planes, chunk, wide), f32),
            pltpu.VMEM((members, chunk, wide), f32),
            pltpu.VMEM((members, right, wide), f32),
            pltpu.VMEM((planes, right, wide), f32),
            pltpu.VMEM((wide, half), bf16),
            pltpu.VMEM((wide, half), bf16),
            pltpu.VMEM((lanes, half), bf16),
            pltpu.VMEM((lanes, half), bf16),
            pltpu.VMEM((lanes, half), bf16),
            pltpu.VMEM((lanes, half), bf16),
            dma((6,)),
            dma((BLOCKS + 1,)),
            dma((LEVELS, 2)),
            dma((LEVELS, 2)),
            dma((LEVELS, 2)),
            dma((LEVELS, 2)),
            dma((LEVELS, 2)),
            dma((LEVELS, 2)),
            dma((2,)),
            dma((2,)),
            dma((4,)),
            dma((4,)),
            dma,
            dma,
            dma((LEVELS,)),
            dma((LEVELS,)),
            dma((3,)),
            dma((3,)),
            dma,
            dma,
            dma,
            dma,
        ],
        compiler_params=pltpu.CompilerParams(
            collective_id=0, has_side_effects=True, vmem_limit_bytes=60 * 1024 * 1024
        ),
    )(bounds, residual, local_inverse, corner_basis, corner_map, coarse_inverse)


def solution(mesh):
    in_specs = (
        P(None, "sub", "grp", None),
        P(),
        P("sub", "grp", None, None),
        P("sub", "grp", None, None),
        P("sub", "grp", None),
        P(("sub", "grp"), None),
    )
    out_specs = (P(None, None, "sub", "grp", None), P())
    run = functools.partial(body, mesh.shape["sub"], mesh.shape["grp"])
    return jax.shard_map(run, mesh=mesh, in_specs=in_specs, out_specs=out_specs, check_vma=False)
```

```python
import functools

import jax
import jax.numpy as jnp
from jax import lax
from jax.experimental import pallas as pl
from jax.experimental.pallas import tpu as pltpu
from jax.sharding import PartitionSpec as P

S_STEP = 2
BLOCKS = 2 * S_STEP + 1
LEVELS = 2 * S_STEP
LOGICAL = pl.DeviceIdType.LOGICAL
HIGHEST = lax.Precision.HIGHEST


def exact(a, b):
    return jnp.dot(a, b, precision=HIGHEST, preferred_element_type=jnp.float32)


def across_rows(a, b, precision=None):
    return lax.dot_general(
        a, b, (((1,), (1,)), ((), ())), precision=precision, preferred_element_type=jnp.float32
    )


def dot(a, b):
    return jnp.dot(a, b, preferred_element_type=jnp.float32)


def kernel(
    nsub, ngrp, inner, pack,
    bounds_hbm, res_hbm, inv_hbm, corner_hbm, map_hbm, coarse_hbm,
    basis_hbm, gram_hbm,
    basis_ref, gram_ref, bounds, res, inv, corner, ids_ref,
    up_out, up_in, diag_in, low_out, low_in, term_out, term_in, edge, cross,
    rows_c, direct, part_out, part_near, part_far, part_all, near, far,
    high, rest, load_high, load_rest, lift_high, lift_rest,
    load_sem, store_sem, up_send, up_recv, diag_send, diag_recv, low_send, low_recv,
    term_send, term_recv, edge_send, edge_recv, rows_send, rows_recv, direct_send, direct_recv,
    part_send, part_recv, near_send, near_recv, far_send, far_recv,
):
    right, half = up_out.shape[2], high.shape[1]
    face = half // 2
    order = BLOCKS * right
    nco = rows_c.shape[2]
    planes = nsub // inner
    members = inner * ngrp
    devices = nsub * ngrp
    packed_rows = right // pack
    chunk = part_out.shape[1]
    sub = lax.axis_index("sub")
    grp = lax.axis_index("grp")
    me = sub * ngrp + grp
    plane = lax.div(sub, inner)
    within = lax.rem(sub, inner)
    member = within * ngrp + grp
    sub_up, sub_down = lax.rem(sub + 1, nsub), lax.rem(sub + nsub - 1, nsub)
    grp_up, grp_down = lax.rem(grp + 1, ngrp), lax.rem(grp + ngrp - 1, ngrp)
    next_sub, prev_sub = sub_up * ngrp + grp, sub_down * ngrp + grp
    next_grp, prev_grp = sub * ngrp + grp_up, sub * ngrp + grp_down
    diagonal_peers = (sub_up * ngrp + grp_down, sub_down * ngrp + grp_up)

    def to_all(action):
        def step(offset, carry):
            other = me + offset
            action(jnp.where(other >= devices, other - devices, other))
            return carry

        lax.fori_loop(1, devices, step, 0, unroll=devices <= 64)

    near_others = [lax.rem(member + o, members) for o in range(1, members)]
    near_peers = [plane * members + o for o in near_others]
    far_peers = [lax.rem(plane + o, planes) * members + member for o in range(1, planes)]

    barrier = pltpu.get_barrier_semaphore()
    loads = [
        pltpu.make_async_copy(src, dst, load_sem.at[i])
        for i, (src, dst) in enumerate((
            (corner_hbm, corner),
            (map_hbm, ids_ref),
            (res_hbm, res),
            (coarse_hbm, rows_c.at[me]),
            (bounds_hbm, bounds),
            (inv_hbm.at[0, 0], inv),
        ))
    ]
    for copy in loads[:3]:
        copy.start()
    to_all(lambda peer: pl.semaphore_signal(barrier, inc=1, device_id=peer, device_id_type=LOGICAL))

    for copy in loads[3:]:
        copy.start()

    def send(src, dst, send_sem, recv_sem, peer):
        copy = pltpu.make_async_remote_copy(
            src_ref=src, dst_ref=dst, send_sem=send_sem, recv_sem=recv_sem,
            device_id=peer, device_id_type=LOGICAL,
        )
        copy.start()
        return copy

    pending = []
    stores = []

    def landed(buf, count, send_sem, recv_sem, peer):
        part = buf.at[pl.ds(0, count - 1)]
        copy = pltpu.make_async_remote_copy(
            src_ref=part, dst_ref=part, send_sem=send_sem, recv_sem=recv_sem,
            device_id=peer, device_id_type=LOGICAL,
        )
        copy.wait_recv()
        pending.append(copy)

    def split(value):
        rough = value.astype(jnp.bfloat16)
        return rough, (value - rough.astype(jnp.float32)).astype(jnp.bfloat16)

    def added(buf, count):
        total = buf[0]
        for i in range(1, count):
            total = total + buf[i]
        return total

    def broadcast(buf, slot, peers, send_sem, recv_sem):
        own = buf.at[slot]
        for peer in peers:
            send(own, own, send_sem, recv_sem, peer)

    def send_blocks(place, landing, corners_of):
        copies = [
            send(
                inv.at[pl.ds(first, face), pl.ds(column, face)], landing.at[d],
                edge_send.at[place + d], edge_recv.at[place + d], peer,
            )
            for d, ((first, column), peer) in enumerate(zip(corners_of, (prev_sub, prev_grp)))
        ]
        pending.extend(copies)
        return copies

    high[...] = jnp.zeros_like(high)
    rest[...] = jnp.zeros_like(rest)
    loads[0].wait()
    loads[1].wait()
    ids = ids_ref[0]
    table = (lax.broadcasted_iota(jnp.int32, (nco, ids.shape[1]), 0) == ids).astype(jnp.bfloat16)
    terms = dot(table, corner[0, 0])
    term_out[0] = terms[:, face : 2 * face]
    term_out[1] = terms[:, 3 * face :]
    for copy in loads[2:5]:
        copy.wait()
    x = res[:, 0, 0, :]
    centre = (bounds[0] + bounds[1]) / 2.0
    radius = (bounds[1] - bounds[0]) / 2.0
    scale = 1.0 / jnp.full((right, half), radius, jnp.float32)
    lane = lax.broadcasted_iota(jnp.int32, (right, pack * nco), 1)
    row = lax.broadcasted_iota(jnp.int32, (right, pack * nco), 0)
    mine = lax.div(lane, nco) == lax.div(row, packed_rows)

    def gram_part(first, second):
        both = across_rows(jnp.concatenate([first, second], axis=0), high[...])
        count = first.shape[0]
        return both[:count] + (both[count:] + across_rows(first, rest[...]))

    def coarse_part(packed):
        part = across_rows(packed, load_high[...]) + across_rows(packed, load_rest[...])
        if pack == 1:
            return part
        part = jnp.where(mine, part, 0.0)
        total = part[:packed_rows]
        for q in range(1, pack):
            total = total + part[q * packed_rows : (q + 1) * packed_rows]
        return total

    def coarse_lift(total):
        if pack > 1:
            total = jnp.where(mine, jnp.concatenate([total] * pack, axis=0), 0.0)
        total_high, total_rest = split(total)
        both = dot(jnp.concatenate([total_high, total_rest], axis=0), lift_high[...])
        return both[:right] + (both[right:] + dot(total_high, lift_rest[...]))

    def send_coarse(level, part):
        direct[level, me] = part
        own = direct.at[level, me]
        to_all(lambda peer: send(own, own, direct_send.at[level], direct_recv.at[level], peer))

    def keep(level, value):
        packed, remainder = split(value)
        basis_ref[level, :, 0, 0, :] = value
        high[pl.ds(level * right, right), :] = packed
        rest[pl.ds(level * right, right), :] = remainder
        stores.append(pltpu.make_async_copy(basis_ref.at[level], basis_hbm.at[level], store_sem.at[level]))
        stores[-1].start()
        return packed, remainder

    pl.semaphore_wait(barrier, devices - 1)
    term_copies = [
        send(term_out.at[d], term_in.at[d], term_send.at[d], term_recv.at[d], peer)
        for d, peer in enumerate((prev_sub, prev_grp))
    ]
    pending += term_copies

    previous = None
    for level in range(LEVELS):
        packed = x.astype(jnp.bfloat16)
        x_sub, x_grp = packed[:, :face], packed[:, face:]
        up_out[level, 0] = x_sub
        up_out[level, 1] = x_grp
        ups = [
            send(up_out.at[level, d], up_in.at[level, d], up_send.at[level, d], up_recv.at[level, d], peer)
            for d, peer in enumerate((next_sub, next_grp))
        ]
        diags = [
            send(up_out.at[level, d], diag_in.at[level, d], diag_send.at[level, d], diag_recv.at[level, d], peer)
            for d, peer in enumerate(diagonal_peers)
        ] if level > 0 else []
        pending += ups + diags
        if level > 0:
            part = coarse_part(packed)
        else:
            own = rows_c.at[me]
            to_all(lambda peer: send(own, own, rows_send, rows_recv, peer))
            loads[5].wait()
            blocks = send_blocks(0, edge, ((face, face), (3 * face, 3 * face)))

        def own_part(first):
            columns = slice(first, first + face)
            return dot(x_sub, inv[:face, columns]) + dot(x_grp, inv[2 * face : 3 * face, columns])

        def low_part(value, first, column):
            return dot(value, inv[first : first + face, column : column + face])

        def send_lows(first, second):
            low_out[level, 0] = first
            low_out[level, 1] = second
            copies = [
                send(low_out.at[level, d], low_in.at[level, d], low_send.at[level, d], low_recv.at[level, d], peer)
                for d, peer in enumerate((prev_sub, prev_grp))
            ]
            pending.extend(copies)
            return copies

        first_low, second_low = own_part(face), own_part(3 * face)
        if level > 0:
            lows = send_lows(first_low, second_low)
        else:
            for copy in term_copies:
                copy.wait_recv()
            weight = jnp.concatenate(
                [terms[:, :face] - term_in[0], terms[:, 2 * face : 3 * face] - term_in[1]], axis=1
            )
            weight_high, weight_rest = split(weight)
            load_high[...] = jnp.concatenate([weight_high] * pack, axis=0)
            load_rest[...] = jnp.concatenate([weight_rest] * pack, axis=0)
            part = coarse_part(packed)
        send_coarse(level, part)
        if level == 0:
            for copy in ups:
                copy.wait_recv()
            low_sub, low_grp = up_in[level, 0], up_in[level, 1]
            lows = send_lows(
                first_low - low_part(low_sub, face, face) - low_part(low_grp, 3 * face, face),
                second_low - low_part(low_sub, face, 3 * face) - low_part(low_grp, 3 * face, 3 * face),
            )
            blocks += send_blocks(2, cross, ((3 * face, face), (face, 3 * face)))
        packed, remainder = keep(level, x)
        if level == LEVELS - 1:
            count = LEVELS * right
            first_rows = gram_part(high[:count, :], rest[:count, :])
            for m in range(members):
                part_out[m] = first_rows[m * chunk : (m + 1) * chunk]
            part_near[member] = part_out[member]
            for other, peer in zip(near_others, near_peers):
                send(part_out.at[other], part_near.at[member], part_send.at[0], part_recv.at[0], peer)
        up_sub = own_part(0)
        up_grp = own_part(2 * face)
        if level > 0:
            for copy in ups:
                copy.wait_recv()
            low_sub, low_grp = up_in[level, 0], up_in[level, 1]
        up_sub = up_sub - low_part(low_sub, face, 0) - low_part(low_grp, 3 * face, 0)
        up_grp = up_grp - low_part(low_sub, face, 2 * face) - low_part(low_grp, 3 * face, 2 * face)
        if level == 0:
            landed(rows_c, devices, rows_send, rows_recv, next_grp)
            raised = exact(rows_c[...].reshape(nco, nco), weight)
            raised_high, raised_rest = split(raised)
            lift_high[...] = jnp.concatenate([raised_high] * pack, axis=0)
            lift_rest[...] = jnp.concatenate([raised_rest] * pack, axis=0)
        else:
            if level == 1:
                for copy in blocks:
                    copy.wait_recv()
            up_sub = up_sub + dot(x_sub, edge[0])
            up_grp = up_grp + dot(x_grp, edge[1])
            for copy in diags:
                copy.wait_recv()
            up_sub = up_sub + dot(diag_in[level, 1], cross[0])
            up_grp = up_grp + dot(diag_in[level, 0], cross[1])
        base = jnp.concatenate([up_sub, up_grp], axis=1) - centre * x
        for copy in lows:
            copy.wait_recv()
        base = base - jnp.concatenate([low_in[level, 0], low_in[level, 1]], axis=1)
        landed(direct.at[level], devices, direct_send.at[level], direct_recv.at[level], next_grp)
        image = base + coarse_lift(added(direct.at[level], devices))
        following = image * scale if level == 0 else 2.0 * image * scale - previous
        previous, x = x, following

    packed, remainder = keep(LEVELS, x)
    near[member] = gram_part(packed, remainder)
    broadcast(near, member, near_peers, near_send, near_recv)
    landed(part_near, members, part_send.at[0], part_recv.at[0], near_peers[0])
    part_far[plane] = added(part_near, members)
    broadcast(part_far, plane, far_peers, part_send.at[1], part_recv.at[1])
    landed(near, members, near_send, near_recv, near_peers[0])
    far[plane] = added(near, members)
    broadcast(far, plane, far_peers, far_send, far_recv)
    landed(part_far, planes, part_send.at[1], part_recv.at[1], far_peers[0])
    part_all[member] = added(part_far, planes)
    broadcast(part_all, member, near_peers, part_send.at[2], part_recv.at[2])
    landed(far, planes, far_send, far_recv, far_peers[0])
    last_rows = added(far, planes)
    landed(part_all, members, part_send.at[2], part_recv.at[2], near_peers[0])
    full = jnp.concatenate([part_all[m] for m in range(members)] + [last_rows], axis=0)[:, :order]
    row = lax.broadcasted_iota(jnp.int32, (order, order), 0)
    column = lax.broadcasted_iota(jnp.int32, (order, order), 1)
    below = jnp.where(lax.div(column, right) < lax.div(row, right), full, 0.0)
    same = jnp.where(lax.div(column, right) == lax.div(row, right), full, 0.0)
    gram_ref[...] = (below + same + below.T) * (1.0 / (half * nsub))
    stores.append(pltpu.make_async_copy(gram_ref, gram_hbm, store_sem.at[BLOCKS]))
    stores[-1].start()
    for copy in pending:
        copy.wait_send()
    for copy in stores:
        copy.wait()


def hand_over(basis_from, gram_from, basis_to, gram_to, sems):
    copies = [
        pltpu.make_async_copy(basis_from, basis_to, sems.at[0]),
        pltpu.make_async_copy(gram_from, gram_to, sems.at[1]),
    ]
    for copy in copies:
        copy.start()
    for copy in copies:
        copy.wait()


def body(nsub, ngrp, residual, bounds, local_inverse, corner_basis, corner_map, coarse_inverse):
    right, half = residual.shape[0], residual.shape[3]
    face = half // 2
    width = 4 * face
    rows, nco = coarse_inverse.shape
    order = BLOCKS * right
    devices = nsub * ngrp
    inner = 1
    while nsub % (2 * inner) == 0 and 2 * inner * ngrp <= nsub // inner:
        inner *= 2
    planes, members = nsub // inner, inner * ngrp
    wide = -(-order // 128) * 128
    pack = 128 // nco if nco < 128 and 128 % nco == 0 and right % (128 // nco) == 0 else 1
    lanes = pack * nco
    chunk = LEVELS * right // members
    hbm = pl.BlockSpec(memory_space=pltpu.HBM)
    dma = pltpu.SemaphoreType.DMA
    f32, bf16 = jnp.float32, jnp.bfloat16
    shapes = (
        jax.ShapeDtypeStruct((BLOCKS, right, 1, 1, half), f32),
        jax.ShapeDtypeStruct((order, order), f32),
    )
    limit = 60 * 1024 * 1024
    results = pl.pallas_call(
        functools.partial(kernel, nsub, ngrp, inner, pack),
        out_shape=shapes,
        in_specs=[hbm] * 6,
        out_specs=(hbm, hbm),
        scratch_shapes=[
            pltpu.VMEM((BLOCKS, right, 1, 1, half), f32),
            pltpu.VMEM((order, order), f32),
            pltpu.SMEM(bounds.shape, f32),
            pltpu.VMEM(residual.shape, f32),
            pltpu.VMEM((width, width), bf16),
            pltpu.VMEM(corner_basis.shape, bf16),
            pltpu.VMEM(corner_map.shape, corner_map.dtype),
            pltpu.VMEM((LEVELS, 2, right, face), bf16),
            pltpu.VMEM((LEVELS, 2, right, face), bf16),
            pltpu.VMEM((LEVELS, 2, right, face), bf16),
            pltpu.VMEM((LEVELS, 2, right, face), f32),
            pltpu.VMEM((LEVELS, 2, right, face), f32),
            pltpu.VMEM((2, nco, face), f32),
            pltpu.VMEM((2, nco, face), f32),
            pltpu.VMEM((2, face, face), bf16),
            pltpu.VMEM((2, face, face), bf16),
            pltpu.VMEM((devices, rows, nco), f32),
            pltpu.VMEM((LEVELS, devices, right // pack, lanes), f32),
            pltpu.VMEM((members, chunk, wide), f32),
            pltpu.VMEM((members, chunk, wide), f32),
            pltpu.VMEM((planes, chunk, wide), f32),
            pltpu.VMEM((members, chunk, wide), f32),
            pltpu.VMEM((members, right, wide), f32),
            pltpu.VMEM((planes, right, wide), f32),
            pltpu.VMEM((wide, half), bf16),
            pltpu.VMEM((wide, half), bf16),
            pltpu.VMEM((lanes, half), bf16),
            pltpu.VMEM((lanes, half), bf16),
            pltpu.VMEM((lanes, half), bf16),
            pltpu.VMEM((lanes, half), bf16),
            dma((6,)),
            dma((BLOCKS + 1,)),
            dma((LEVELS, 2)),
            dma((LEVELS, 2)),
            dma((LEVELS, 2)),
            dma((LEVELS, 2)),
            dma((LEVELS, 2)),
            dma((LEVELS, 2)),
            dma((2,)),
            dma((2,)),
            dma((4,)),
            dma((4,)),
            dma,
            dma,
            dma((LEVELS,)),
            dma((LEVELS,)),
            dma((3,)),
            dma((3,)),
            dma,
            dma,
            dma,
            dma,
        ],
        compiler_params=pltpu.CompilerParams(
            collective_id=0, has_side_effects=True, vmem_limit_bytes=limit
        ),
    )(bounds, residual, local_inverse, corner_basis, corner_map, coarse_inverse)
    return pl.pallas_call(
        hand_over,
        out_shape=shapes,
        in_specs=[hbm, hbm],
        out_specs=(hbm, hbm),
        scratch_shapes=[dma((2,))],
        compiler_params=pltpu.CompilerParams(vmem_limit_bytes=limit),
    )(*results)


def solution(mesh):
    in_specs = (
        P(None, "sub", "grp", None),
        P(),
        P("sub", "grp", None, None),
        P("sub", "grp", None, None),
        P("sub", "grp", None),
        P(("sub", "grp"), None),
    )
    out_specs = (P(None, None, "sub", "grp", None), P())
    run = functools.partial(body, mesh.shape["sub"], mesh.shape["grp"])
    return jax.shard_map(run, mesh=mesh, in_specs=in_specs, out_specs=out_specs, check_vma=False)
```

```python
import functools

import jax
import jax.numpy as jnp
from jax import lax
from jax.experimental import pallas as pl
from jax.experimental.pallas import tpu as pltpu
from jax.sharding import PartitionSpec as P

S_STEP = 2
BLOCKS = 2 * S_STEP + 1
LEVELS = 2 * S_STEP
LOGICAL = pl.DeviceIdType.LOGICAL
HIGHEST = lax.Precision.HIGHEST


def exact(a, b):
    return jnp.dot(a, b, precision=HIGHEST, preferred_element_type=jnp.float32)


def across_rows(a, b, precision=None):
    return lax.dot_general(
        a, b, (((1,), (1,)), ((), ())), precision=precision, preferred_element_type=jnp.float32
    )


def dot(a, b):
    return jnp.dot(a, b, preferred_element_type=jnp.float32)


def kernel(
    nsub, ngrp, inner, pack,
    bounds_hbm, res_hbm, inv_hbm, corner_hbm, map_hbm, coarse_hbm,
    basis_hbm, gram_hbm,
    basis_ref, gram_ref, bounds, res, inv, corner, ids_ref,
    up_out, up_in, diag_in, low_out, low_in, term_out, term_in, edge, cross,
    rows_c, direct, part_out, part_near, part_far, part_all, near, far,
    high, rest, load_high, load_rest, lift_high, lift_rest,
    load_sem, store_sem, up_send, up_recv, diag_send, diag_recv, low_send, low_recv,
    term_send, term_recv, edge_send, edge_recv, rows_send, rows_recv, direct_send, direct_recv,
    part_send, part_recv, near_send, near_recv, far_send, far_recv,
):
    right, half = up_out.shape[2], high.shape[1]
    face = half // 2
    order = BLOCKS * right
    nco = rows_c.shape[2]
    planes = nsub // inner
    members = inner * ngrp
    devices = nsub * ngrp
    packed_rows = right // pack
    chunk = part_out.shape[1]
    sub = lax.axis_index("sub")
    grp = lax.axis_index("grp")
    me = sub * ngrp + grp
    plane = lax.div(sub, inner)
    within = lax.rem(sub, inner)
    member = within * ngrp + grp
    sub_up, sub_down = lax.rem(sub + 1, nsub), lax.rem(sub + nsub - 1, nsub)
    grp_up, grp_down = lax.rem(grp + 1, ngrp), lax.rem(grp + ngrp - 1, ngrp)
    next_sub, prev_sub = sub_up * ngrp + grp, sub_down * ngrp + grp
    next_grp, prev_grp = sub * ngrp + grp_up, sub * ngrp + grp_down
    diagonal_peers = (sub_up * ngrp + grp_down, sub_down * ngrp + grp_up)

    def to_all(action):
        def step(offset, carry):
            other = me + offset
            action(jnp.where(other >= devices, other - devices, other))
            return carry

        lax.fori_loop(1, devices, step, 0, unroll=devices <= 64)

    near_others = [lax.rem(member + o, members) for o in range(1, members)]
    near_peers = [plane * members + o for o in near_others]
    far_peers = [lax.rem(plane + o, planes) * members + member for o in range(1, planes)]

    barrier = pltpu.get_barrier_semaphore()
    loads = [
        pltpu.make_async_copy(src, dst, load_sem.at[i])
        for i, (src, dst) in enumerate((
            (corner_hbm, corner),
            (map_hbm, ids_ref),
            (res_hbm, res),
            (coarse_hbm, rows_c.at[me]),
            (bounds_hbm, bounds),
            (inv_hbm.at[0, 0], inv),
        ))
    ]
    for copy in loads[:3]:
        copy.start()
    to_all(lambda peer: pl.semaphore_signal(barrier, inc=1, device_id=peer, device_id_type=LOGICAL))

    for copy in loads[3:]:
        copy.start()

    def send(src, dst, send_sem, recv_sem, peer):
        copy = pltpu.make_async_remote_copy(
            src_ref=src, dst_ref=dst, send_sem=send_sem, recv_sem=recv_sem,
            device_id=peer, device_id_type=LOGICAL,
        )
        copy.start()
        return copy

    pending = []
    stores = []

    def landed(buf, count, send_sem, recv_sem, peer):
        part = buf.at[pl.ds(0, count - 1)]
        copy = pltpu.make_async_remote_copy(
            src_ref=part, dst_ref=part, send_sem=send_sem, recv_sem=recv_sem,
            device_id=peer, device_id_type=LOGICAL,
        )
        copy.wait_recv()
        pending.append(copy)

    def split(value):
        rough = value.astype(jnp.bfloat16)
        return rough, (value - rough.astype(jnp.float32)).astype(jnp.bfloat16)

    def added(buf, count):
        total = buf[0]
        for i in range(1, count):
            total = total + buf[i]
        return total

    def broadcast(buf, slot, peers, send_sem, recv_sem):
        own = buf.at[slot]
        for peer in peers:
            send(own, own, send_sem, recv_sem, peer)

    def send_blocks(place, landing, corners_of):
        copies = [
            send(
                inv.at[pl.ds(first, face), pl.ds(column, face)], landing.at[d],
                edge_send.at[place + d], edge_recv.at[place + d], peer,
            )
            for d, ((first, column), peer) in enumerate(zip(corners_of, (prev_sub, prev_grp)))
        ]
        pending.extend(copies)
        return copies

    high[...] = jnp.zeros_like(high)
    rest[...] = jnp.zeros_like(rest)
    loads[0].wait()
    loads[1].wait()
    ids = ids_ref[0]
    table = (lax.broadcasted_iota(jnp.int32, (nco, ids.shape[1]), 0) == ids).astype(jnp.bfloat16)
    terms = dot(table, corner[0, 0])
    term_out[0] = terms[:, face : 2 * face]
    term_out[1] = terms[:, 3 * face :]
    for copy in loads[2:5]:
        copy.wait()
    x = res[:, 0, 0, :]
    centre = (bounds[0] + bounds[1]) / 2.0
    radius = (bounds[1] - bounds[0]) / 2.0
    scale = 1.0 / jnp.full((right, half), radius, jnp.float32)
    lane = lax.broadcasted_iota(jnp.int32, (right, pack * nco), 1)
    row = lax.broadcasted_iota(jnp.int32, (right, pack * nco), 0)
    mine = lax.div(lane, nco) == lax.div(row, packed_rows)

    def gram_part(first, second):
        both = across_rows(jnp.concatenate([first, second], axis=0), high[...])
        count = first.shape[0]
        return both[:count] + (both[count:] + across_rows(first, rest[...]))

    def coarse_part(packed):
        part = across_rows(packed, load_high[...]) + across_rows(packed, load_rest[...])
        if pack == 1:
            return part
        part = jnp.where(mine, part, 0.0)
        total = part[:packed_rows]
        for q in range(1, pack):
            total = total + part[q * packed_rows : (q + 1) * packed_rows]
        return total

    def coarse_lift(total):
        if pack > 1:
            total = jnp.where(mine, jnp.concatenate([total] * pack, axis=0), 0.0)
        total_high, total_rest = split(total)
        both = dot(jnp.concatenate([total_high, total_rest], axis=0), lift_high[...])
        return both[:right] + (both[right:] + dot(total_high, lift_rest[...]))

    def send_coarse(level, part):
        direct[level, me] = part
        own = direct.at[level, me]
        to_all(lambda peer: send(own, own, direct_send.at[level], direct_recv.at[level], peer))

    def keep(level, value):
        packed, remainder = split(value)
        basis_ref[level] = value
        high[pl.ds(level * right, right), :] = packed
        rest[pl.ds(level * right, right), :] = remainder
        stores.append(pltpu.make_async_copy(basis_ref.at[level], basis_hbm.at[level], store_sem.at[level]))
        stores[-1].start()
        return packed, remainder

    pl.semaphore_wait(barrier, devices - 1)
    term_copies = [
        send(term_out.at[d], term_in.at[d], term_send.at[d], term_recv.at[d], peer)
        for d, peer in enumerate((prev_sub, prev_grp))
    ]
    pending += term_copies

    previous = None
    for level in range(LEVELS):
        packed = x.astype(jnp.bfloat16)
        x_sub, x_grp = packed[:, :face], packed[:, face:]
        up_out[level, 0] = x_sub
        up_out[level, 1] = x_grp
        ups = [
            send(up_out.at[level, d], up_in.at[level, d], up_send.at[level, d], up_recv.at[level, d], peer)
            for d, peer in enumerate((next_sub, next_grp))
        ]
        diags = [
            send(up_out.at[level, d], diag_in.at[level, d], diag_send.at[level, d], diag_recv.at[level, d], peer)
            for d, peer in enumerate(diagonal_peers)
        ] if level > 0 else []
        pending += ups + diags
        if level > 0:
            part = coarse_part(packed)
        else:
            own = rows_c.at[me]
            to_all(lambda peer: send(own, own, rows_send, rows_recv, peer))
            loads[5].wait()
            blocks = send_blocks(0, edge, ((face, face), (3 * face, 3 * face)))

        def own_part(first):
            columns = slice(first, first + face)
            return dot(x_sub, inv[:face, columns]) + dot(x_grp, inv[2 * face : 3 * face, columns])

        def low_part(value, first, column):
            return dot(value, inv[first : first + face, column : column + face])

        def send_lows(first, second):
            low_out[level, 0] = first
            low_out[level, 1] = second
            copies = [
                send(low_out.at[level, d], low_in.at[level, d], low_send.at[level, d], low_recv.at[level, d], peer)
                for d, peer in enumerate((prev_sub, prev_grp))
            ]
            pending.extend(copies)
            return copies

        first_low, second_low = own_part(face), own_part(3 * face)
        if level > 0:
            lows = send_lows(first_low, second_low)
        else:
            for copy in term_copies:
                copy.wait_recv()
            weight = jnp.concatenate(
                [terms[:, :face] - term_in[0], terms[:, 2 * face : 3 * face] - term_in[1]], axis=1
            )
            weight_high, weight_rest = split(weight)
            load_high[...] = jnp.concatenate([weight_high] * pack, axis=0)
            load_rest[...] = jnp.concatenate([weight_rest] * pack, axis=0)
            part = coarse_part(packed)
        send_coarse(level, part)
        if level == 0:
            for copy in ups:
                copy.wait_recv()
            low_sub, low_grp = up_in[level, 0], up_in[level, 1]
            lows = send_lows(
                first_low - low_part(low_sub, face, face) - low_part(low_grp, 3 * face, face),
                second_low - low_part(low_sub, face, 3 * face) - low_part(low_grp, 3 * face, 3 * face),
            )
            blocks += send_blocks(2, cross, ((3 * face, face), (face, 3 * face)))
        packed, remainder = keep(level, x)
        if level == LEVELS - 1:
            count = LEVELS * right
            first_rows = gram_part(high[:count, :], rest[:count, :])
            for m in range(members):
                part_out[m] = first_rows[m * chunk : (m + 1) * chunk]
            part_near[member] = part_out[member]
            for other, peer in zip(near_others, near_peers):
                send(part_out.at[other], part_near.at[member], part_send.at[0], part_recv.at[0], peer)
        up_sub = own_part(0)
        up_grp = own_part(2 * face)
        if level > 0:
            for copy in ups:
                copy.wait_recv()
            low_sub, low_grp = up_in[level, 0], up_in[level, 1]
        up_sub = up_sub - low_part(low_sub, face, 0) - low_part(low_grp, 3 * face, 0)
        up_grp = up_grp - low_part(low_sub, face, 2 * face) - low_part(low_grp, 3 * face, 2 * face)
        if level == 0:
            landed(rows_c, devices, rows_send, rows_recv, next_grp)
            raised = exact(rows_c[...].reshape(nco, nco), weight)
            raised_high, raised_rest = split(raised)
            lift_high[...] = jnp.concatenate([raised_high] * pack, axis=0)
            lift_rest[...] = jnp.concatenate([raised_rest] * pack, axis=0)
        else:
            if level == 1:
                for copy in blocks:
                    copy.wait_recv()
            up_sub = up_sub + dot(x_sub, edge[0])
            up_grp = up_grp + dot(x_grp, edge[1])
            for copy in diags:
                copy.wait_recv()
            up_sub = up_sub + dot(diag_in[level, 1], cross[0])
            up_grp = up_grp + dot(diag_in[level, 0], cross[1])
        base = jnp.concatenate([up_sub, up_grp], axis=1) - centre * x
        for copy in lows:
            copy.wait_recv()
        base = base - jnp.concatenate([low_in[level, 0], low_in[level, 1]], axis=1)
        landed(direct.at[level], devices, direct_send.at[level], direct_recv.at[level], next_grp)
        image = base + coarse_lift(added(direct.at[level], devices))
        following = image * scale if level == 0 else 2.0 * image * scale - previous
        previous, x = x, following

    packed, remainder = keep(LEVELS, x)
    near[member] = gram_part(packed, remainder)
    broadcast(near, member, near_peers, near_send, near_recv)
    landed(part_near, members, part_send.at[0], part_recv.at[0], near_peers[0])
    part_far[plane] = added(part_near, members)
    broadcast(part_far, plane, far_peers, part_send.at[1], part_recv.at[1])
    landed(near, members, near_send, near_recv, near_peers[0])
    far[plane] = added(near, members)
    broadcast(far, plane, far_peers, far_send, far_recv)
    landed(part_far, planes, part_send.at[1], part_recv.at[1], far_peers[0])
    part_all[member] = added(part_far, planes)
    broadcast(part_all, member, near_peers, part_send.at[2], part_recv.at[2])
    landed(far, planes, far_send, far_recv, far_peers[0])
    last_rows = added(far, planes)
    landed(part_all, members, part_send.at[2], part_recv.at[2], near_peers[0])
    full = jnp.concatenate([part_all[m] for m in range(members)] + [last_rows], axis=0)[:, :order]
    row = lax.broadcasted_iota(jnp.int32, (order, order), 0)
    column = lax.broadcasted_iota(jnp.int32, (order, order), 1)
    below = jnp.where(lax.div(column, right) < lax.div(row, right), full, 0.0)
    same = jnp.where(lax.div(column, right) == lax.div(row, right), full, 0.0)
    gram_ref[...] = below + same + below.T
    stores.append(pltpu.make_async_copy(gram_ref, gram_hbm, store_sem.at[BLOCKS]))
    stores[-1].start()
    for copy in pending:
        copy.wait_send()
    for copy in stores:
        copy.wait()


def body(nsub, ngrp, residual, bounds, local_inverse, corner_basis, corner_map, coarse_inverse):
    right, half = residual.shape[0], residual.shape[3]
    face = half // 2
    width = 4 * face
    rows, nco = coarse_inverse.shape
    order = BLOCKS * right
    devices = nsub * ngrp
    inner = 1
    while nsub % (2 * inner) == 0 and 2 * inner * ngrp <= nsub // inner:
        inner *= 2
    planes, members = nsub // inner, inner * ngrp
    wide = -(-order // 128) * 128
    pack = 128 // nco if nco < 128 and 128 % nco == 0 and right % (128 // nco) == 0 else 1
    lanes = pack * nco
    chunk = LEVELS * right // members
    hbm = pl.BlockSpec(memory_space=pltpu.HBM)
    dma = pltpu.SemaphoreType.DMA
    f32, bf16 = jnp.float32, jnp.bfloat16
    basis, gram = pl.pallas_call(
        functools.partial(kernel, nsub, ngrp, inner, pack),
        out_shape=(
            jax.ShapeDtypeStruct((BLOCKS, right, half), f32),
            jax.ShapeDtypeStruct((order, order), f32),
        ),
        in_specs=[hbm] * 6,
        out_specs=(hbm, hbm),
        scratch_shapes=[
            pltpu.VMEM((BLOCKS, right, half), f32),
            pltpu.VMEM((order, order), f32),
            pltpu.SMEM(bounds.shape, f32),
            pltpu.VMEM(residual.shape, f32),
            pltpu.VMEM((width, width), bf16),
            pltpu.VMEM(corner_basis.shape, bf16),
            pltpu.VMEM(corner_map.shape, corner_map.dtype),
            pltpu.VMEM((LEVELS, 2, right, face), bf16),
            pltpu.VMEM((LEVELS, 2, right, face), bf16),
            pltpu.VMEM((LEVELS, 2, right, face), bf16),
            pltpu.VMEM((LEVELS, 2, right, face), f32),
            pltpu.VMEM((LEVELS, 2, right, face), f32),
            pltpu.VMEM((2, nco, face), f32),
            pltpu.VMEM((2, nco, face), f32),
            pltpu.VMEM((2, face, face), bf16),
            pltpu.VMEM((2, face, face), bf16),
            pltpu.VMEM((devices, rows, nco), f32),
            pltpu.VMEM((LEVELS, devices, right // pack, lanes), f32),
            pltpu.VMEM((members, chunk, wide), f32),
            pltpu.VMEM((members, chunk, wide), f32),
            pltpu.VMEM((planes, chunk, wide), f32),
            pltpu.VMEM((members, chunk, wide), f32),
            pltpu.VMEM((members, right, wide), f32),
            pltpu.VMEM((planes, right, wide), f32),
            pltpu.VMEM((wide, half), bf16),
            pltpu.VMEM((wide, half), bf16),
            pltpu.VMEM((lanes, half), bf16),
            pltpu.VMEM((lanes, half), bf16),
            pltpu.VMEM((lanes, half), bf16),
            pltpu.VMEM((lanes, half), bf16),
            dma((6,)),
            dma((BLOCKS + 1,)),
            dma((LEVELS, 2)),
            dma((LEVELS, 2)),
            dma((LEVELS, 2)),
            dma((LEVELS, 2)),
            dma((LEVELS, 2)),
            dma((LEVELS, 2)),
            dma((2,)),
            dma((2,)),
            dma((4,)),
            dma((4,)),
            dma,
            dma,
            dma((LEVELS,)),
            dma((LEVELS,)),
            dma((3,)),
            dma((3,)),
            dma,
            dma,
            dma,
            dma,
        ],
        compiler_params=pltpu.CompilerParams(
            collective_id=0, has_side_effects=True, vmem_limit_bytes=60 * 1024 * 1024
        ),
    )(bounds, residual, local_inverse, corner_basis, corner_map, coarse_inverse)
    return basis.reshape(BLOCKS, right, 1, 1, half), gram * (1.0 / (half * nsub))


def solution(mesh):
    in_specs = (
        P(None, "sub", "grp", None),
        P(),
        P("sub", "grp", None, None),
        P("sub", "grp", None, None),
        P("sub", "grp", None),
        P(("sub", "grp"), None),
    )
    out_specs = (P(None, None, "sub", "grp", None), P())
    run = functools.partial(body, mesh.shape["sub"], mesh.shape["grp"])
    return jax.shard_map(run, mesh=mesh, in_specs=in_specs, out_specs=out_specs, check_vma=False)
```

```python
import functools

import jax
import jax.numpy as jnp
from jax import lax
from jax.experimental import pallas as pl
from jax.experimental.pallas import tpu as pltpu
from jax.sharding import PartitionSpec as P

S_STEP = 2
BLOCKS = 2 * S_STEP + 1
LEVELS = 2 * S_STEP
LOGICAL = pl.DeviceIdType.LOGICAL
HIGHEST = lax.Precision.HIGHEST


def exact(a, b):
    return jnp.dot(a, b, precision=HIGHEST, preferred_element_type=jnp.float32)


def across_rows(a, b, precision=None):
    return lax.dot_general(
        a, b, (((1,), (1,)), ((), ())), precision=precision, preferred_element_type=jnp.float32
    )


def dot(a, b):
    return jnp.dot(a, b, preferred_element_type=jnp.float32)


def kernel(
    nsub, ngrp, inner, pack,
    bounds_hbm, res_hbm, inv_hbm, corner_hbm, map_hbm, coarse_hbm,
    basis_hbm, gram_hbm,
    basis_ref, gram_ref, bounds, res, inv, corner, ids_ref,
    up_out, up_in, diag_in, low_out, low_in, term_out, term_in, edge, cross,
    rows_c, direct, part_out, part_near, part_far, part_all, near, far,
    high, rest, load_high, load_rest, lift_high, lift_rest,
    load_sem, store_sem, up_send, up_recv, diag_send, diag_recv, low_send, low_recv,
    term_send, term_recv, edge_send, edge_recv, rows_send, rows_recv, direct_send, direct_recv,
    part_send, part_recv, near_send, near_recv, far_send, far_recv,
):
    right, half = up_out.shape[2], high.shape[1]
    face = half // 2
    order = BLOCKS * right
    nco = rows_c.shape[2]
    planes = nsub // inner
    members = inner * ngrp
    devices = nsub * ngrp
    packed_rows = right // pack
    chunk = part_out.shape[1]
    sub = lax.axis_index("sub")
    grp = lax.axis_index("grp")
    me = sub * ngrp + grp
    plane = lax.div(sub, inner)
    within = lax.rem(sub, inner)
    member = within * ngrp + grp
    sub_up, sub_down = lax.rem(sub + 1, nsub), lax.rem(sub + nsub - 1, nsub)
    grp_up, grp_down = lax.rem(grp + 1, ngrp), lax.rem(grp + ngrp - 1, ngrp)
    next_sub, prev_sub = sub_up * ngrp + grp, sub_down * ngrp + grp
    next_grp, prev_grp = sub * ngrp + grp_up, sub * ngrp + grp_down
    diagonal_peers = (sub_up * ngrp + grp_down, sub_down * ngrp + grp_up)

    def to_all(action):
        def step(offset, carry):
            other = me + offset
            action(jnp.where(other >= devices, other - devices, other))
            return carry

        lax.fori_loop(members, devices, step, 0, unroll=devices <= 64)
        lax.fori_loop(1, members, step, 0, unroll=devices <= 64)

    near_others = [lax.rem(member + o, members) for o in range(1, members)]
    near_peers = [plane * members + o for o in near_others]
    far_peers = [lax.rem(plane + o, planes) * members + member for o in range(1, planes)]

    barrier = pltpu.get_barrier_semaphore()
    loads = [
        pltpu.make_async_copy(src, dst, load_sem.at[i])
        for i, (src, dst) in enumerate((
            (corner_hbm, corner),
            (map_hbm, ids_ref),
            (res_hbm, res),
            (coarse_hbm, rows_c.at[me]),
            (bounds_hbm, bounds),
            (inv_hbm.at[0, 0], inv),
        ))
    ]
    for copy in loads:
        copy.start()
    to_all(lambda peer: pl.semaphore_signal(barrier, inc=1, device_id=peer, device_id_type=LOGICAL))

    def send(src, dst, send_sem, recv_sem, peer):
        copy = pltpu.make_async_remote_copy(
            src_ref=src, dst_ref=dst, send_sem=send_sem, recv_sem=recv_sem,
            device_id=peer, device_id_type=LOGICAL,
        )
        copy.start()
        return copy

    pending = []
    stores = []

    def landed(buf, count, send_sem, recv_sem, peer):
        part = buf.at[pl.ds(0, count - 1)]
        copy = pltpu.make_async_remote_copy(
            src_ref=part, dst_ref=part, send_sem=send_sem, recv_sem=recv_sem,
            device_id=peer, device_id_type=LOGICAL,
        )
        copy.wait_recv()
        pending.append(copy)

    def split(value):
        rough = value.astype(jnp.bfloat16)
        return rough, (value - rough.astype(jnp.float32)).astype(jnp.bfloat16)

    def added(buf, count):
        total = buf[0]
        for i in range(1, count):
            total = total + buf[i]
        return total

    def broadcast(buf, slot, peers, send_sem, recv_sem):
        own = buf.at[slot]
        for peer in peers:
            send(own, own, send_sem, recv_sem, peer)

    def send_blocks(place, landing, corners_of):
        copies = [
            send(
                inv.at[pl.ds(first, face), pl.ds(column, face)], landing.at[d],
                edge_send.at[place + d], edge_recv.at[place + d], peer,
            )
            for d, ((first, column), peer) in enumerate(zip(corners_of, (prev_sub, prev_grp)))
        ]
        pending.extend(copies)
        return copies

    high[...] = jnp.zeros_like(high)
    rest[...] = jnp.zeros_like(rest)
    loads[0].wait()
    loads[1].wait()
    ids = ids_ref[0]
    table = (lax.broadcasted_iota(jnp.int32, (nco, ids.shape[1]), 0) == ids).astype(jnp.bfloat16)
    terms = dot(table, corner[0, 0])
    term_out[0] = terms[:, face : 2 * face]
    term_out[1] = terms[:, 3 * face :]
    for copy in loads[2:5]:
        copy.wait()
    x = res[:, 0, 0, :]
    centre = (bounds[0] + bounds[1]) / 2.0
    radius = (bounds[1] - bounds[0]) / 2.0
    scale = 1.0 / jnp.full((right, half), radius, jnp.float32)
    lane = lax.broadcasted_iota(jnp.int32, (right, pack * nco), 1)
    row = lax.broadcasted_iota(jnp.int32, (right, pack * nco), 0)
    mine = lax.div(lane, nco) == lax.div(row, packed_rows)

    def gram_part(first, second):
        both = across_rows(jnp.concatenate([first, second], axis=0), high[...])
        count = first.shape[0]
        return both[:count] + (both[count:] + across_rows(first, rest[...]))

    def coarse_part(packed):
        part = across_rows(packed, load_high[...]) + across_rows(packed, load_rest[...])
        if pack == 1:
            return part
        part = jnp.where(mine, part, 0.0)
        total = part[:packed_rows]
        for q in range(1, pack):
            total = total + part[q * packed_rows : (q + 1) * packed_rows]
        return total

    def coarse_lift(total):
        if pack > 1:
            total = jnp.where(mine, jnp.concatenate([total] * pack, axis=0), 0.0)
        total_high, total_rest = split(total)
        both = dot(jnp.concatenate([total_high, total_rest], axis=0), lift_high[...])
        return both[:right] + (both[right:] + dot(total_high, lift_rest[...]))

    def send_coarse(level, part):
        direct[level, me] = part
        own = direct.at[level, me]
        to_all(lambda peer: send(own, own, direct_send.at[level], direct_recv.at[level], peer))

    def keep(level, value):
        packed, remainder = split(value)
        basis_ref[level, :, 0, 0, :] = value
        high[pl.ds(level * right, right), :] = packed
        rest[pl.ds(level * right, right), :] = remainder
        stores.append(pltpu.make_async_copy(basis_ref.at[level], basis_hbm.at[level], store_sem.at[level]))
        stores[-1].start()
        return packed, remainder

    pl.semaphore_wait(barrier, devices - 1)
    term_copies = [
        send(term_out.at[d], term_in.at[d], term_send.at[d], term_recv.at[d], peer)
        for d, peer in enumerate((prev_sub, prev_grp))
    ]
    pending += term_copies

    previous = None
    for level in range(LEVELS):
        packed = x.astype(jnp.bfloat16)
        x_sub, x_grp = packed[:, :face], packed[:, face:]
        up_out[level, 0] = x_sub
        up_out[level, 1] = x_grp
        ups = [
            send(up_out.at[level, d], up_in.at[level, d], up_send.at[level, d], up_recv.at[level, d], peer)
            for d, peer in enumerate((next_sub, next_grp))
        ]
        diags = [
            send(up_out.at[level, d], diag_in.at[level, d], diag_send.at[level, d], diag_recv.at[level, d], peer)
            for d, peer in enumerate(diagonal_peers)
        ] if level > 0 else []
        pending += ups + diags
        if level > 0:
            send_coarse(level, coarse_part(packed))
        else:
            own = rows_c.at[me]
            to_all(lambda peer: send(own, own, rows_send, rows_recv, peer))
            loads[5].wait()
            blocks = send_blocks(0, edge, ((face, face), (3 * face, 3 * face)))

        def own_part(first):
            columns = slice(first, first + face)
            return dot(x_sub, inv[:face, columns]) + dot(x_grp, inv[2 * face : 3 * face, columns])

        def low_part(value, first, column):
            return dot(value, inv[first : first + face, column : column + face])

        def send_lows(first, second):
            low_out[level, 0] = first
            low_out[level, 1] = second
            copies = [
                send(low_out.at[level, d], low_in.at[level, d], low_send.at[level, d], low_recv.at[level, d], peer)
                for d, peer in enumerate((prev_sub, prev_grp))
            ]
            pending.extend(copies)
            return copies

        first_low, second_low = own_part(face), own_part(3 * face)
        if level > 0:
            lows = send_lows(first_low, second_low)
        else:
            for copy in term_copies:
                copy.wait_recv()
            weight = jnp.concatenate(
                [terms[:, :face] - term_in[0], terms[:, 2 * face : 3 * face] - term_in[1]], axis=1
            )
            weight_high, weight_rest = split(weight)
            load_high[...] = jnp.concatenate([weight_high] * pack, axis=0)
            load_rest[...] = jnp.concatenate([weight_rest] * pack, axis=0)
            send_coarse(level, coarse_part(packed))
            for copy in ups:
                copy.wait_recv()
            low_sub, low_grp = up_in[level, 0], up_in[level, 1]
            lows = send_lows(
                first_low - low_part(low_sub, face, face) - low_part(low_grp, 3 * face, face),
                second_low - low_part(low_sub, face, 3 * face) - low_part(low_grp, 3 * face, 3 * face),
            )
            blocks += send_blocks(2, cross, ((3 * face, face), (face, 3 * face)))
        packed, remainder = keep(level, x)
        if level == LEVELS - 1:
            count = LEVELS * right
            first_rows = gram_part(high[:count, :], rest[:count, :])
            for m in range(members):
                part_out[m] = first_rows[m * chunk : (m + 1) * chunk]
            part_near[member] = part_out[member]
            for other, peer in zip(near_others, near_peers):
                send(part_out.at[other], part_near.at[member], part_send.at[0], part_recv.at[0], peer)
        up_sub = own_part(0)
        up_grp = own_part(2 * face)
        if level > 0:
            for copy in ups:
                copy.wait_recv()
            low_sub, low_grp = up_in[level, 0], up_in[level, 1]
        up_sub = up_sub - low_part(low_sub, face, 0) - low_part(low_grp, 3 * face, 0)
        up_grp = up_grp - low_part(low_sub, face, 2 * face) - low_part(low_grp, 3 * face, 2 * face)
        if level == 0:
            landed(rows_c, devices, rows_send, rows_recv, next_grp)
            raised = exact(rows_c[...].reshape(nco, nco), weight)
            raised_high, raised_rest = split(raised)
            lift_high[...] = jnp.concatenate([raised_high] * pack, axis=0)
            lift_rest[...] = jnp.concatenate([raised_rest] * pack, axis=0)
        else:
            if level == 1:
                for copy in blocks:
                    copy.wait_recv()
            up_sub = up_sub + dot(x_sub, edge[0])
            up_grp = up_grp + dot(x_grp, edge[1])
            for copy in diags:
                copy.wait_recv()
            up_sub = up_sub + dot(diag_in[level, 1], cross[0])
            up_grp = up_grp + dot(diag_in[level, 0], cross[1])
        base = jnp.concatenate([up_sub, up_grp], axis=1) - centre * x
        for copy in lows:
            copy.wait_recv()
        base = base - jnp.concatenate([low_in[level, 0], low_in[level, 1]], axis=1)
        landed(direct.at[level], devices, direct_send.at[level], direct_recv.at[level], next_grp)
        image = base + coarse_lift(added(direct.at[level], devices))
        following = image * scale if level == 0 else 2.0 * image * scale - previous
        previous, x = x, following

    packed, remainder = keep(LEVELS, x)
    near[member] = gram_part(packed, remainder)
    broadcast(near, member, near_peers, near_send, near_recv)
    landed(part_near, members, part_send.at[0], part_recv.at[0], near_peers[0])
    part_far[plane] = added(part_near, members)
    broadcast(part_far, plane, far_peers, part_send.at[1], part_recv.at[1])
    landed(near, members, near_send, near_recv, near_peers[0])
    far[plane] = added(near, members)
    broadcast(far, plane, far_peers, far_send, far_recv)
    landed(part_far, planes, part_send.at[1], part_recv.at[1], far_peers[0])
    part_all[member] = added(part_far, planes)
    broadcast(part_all, member, near_peers, part_send.at[2], part_recv.at[2])
    landed(far, planes, far_send, far_recv, far_peers[0])
    last_rows = added(far, planes)
    landed(part_all, members, part_send.at[2], part_recv.at[2], near_peers[0])
    full = jnp.concatenate([part_all[m] for m in range(members)] + [last_rows], axis=0)[:, :order]
    row = lax.broadcasted_iota(jnp.int32, (order, order), 0)
    column = lax.broadcasted_iota(jnp.int32, (order, order), 1)
    below = jnp.where(lax.div(column, right) < lax.div(row, right), full, 0.0)
    same = jnp.where(lax.div(column, right) == lax.div(row, right), full, 0.0)
    gram_ref[...] = (below + same + below.T) * (1.0 / (half * nsub))
    stores.append(pltpu.make_async_copy(gram_ref, gram_hbm, store_sem.at[BLOCKS]))
    stores[-1].start()
    for copy in pending:
        copy.wait_send()
    for copy in stores:
        copy.wait()


def body(nsub, ngrp, residual, bounds, local_inverse, corner_basis, corner_map, coarse_inverse):
    right, half = residual.shape[0], residual.shape[3]
    face = half // 2
    width = 4 * face
    rows, nco = coarse_inverse.shape
    order = BLOCKS * right
    devices = nsub * ngrp
    inner = 1
    while nsub % (2 * inner) == 0 and 2 * inner * ngrp <= nsub // inner:
        inner *= 2
    planes, members = nsub // inner, inner * ngrp
    wide = -(-order // 128) * 128
    pack = 128 // nco if nco < 128 and 128 % nco == 0 and right % (128 // nco) == 0 else 1
    lanes = pack * nco
    chunk = LEVELS * right // members
    hbm = pl.BlockSpec(memory_space=pltpu.HBM)
    dma = pltpu.SemaphoreType.DMA
    f32, bf16 = jnp.float32, jnp.bfloat16
    return pl.pallas_call(
        functools.partial(kernel, nsub, ngrp, inner, pack),
        out_shape=(
            jax.ShapeDtypeStruct((BLOCKS, right, 1, 1, half), f32),
            jax.ShapeDtypeStruct((order, order), f32),
        ),
        in_specs=[hbm] * 6,
        out_specs=(hbm, hbm),
        scratch_shapes=[
            pltpu.VMEM((BLOCKS, right, 1, 1, half), f32),
            pltpu.VMEM((order, order), f32),
            pltpu.SMEM(bounds.shape, f32),
            pltpu.VMEM(residual.shape, f32),
            pltpu.VMEM((width, width), bf16),
            pltpu.VMEM(corner_basis.shape, bf16),
            pltpu.VMEM(corner_map.shape, corner_map.dtype),
            pltpu.VMEM((LEVELS, 2, right, face), bf16),
            pltpu.VMEM((LEVELS, 2, right, face), bf16),
            pltpu.VMEM((LEVELS, 2, right, face), bf16),
            pltpu.VMEM((LEVELS, 2, right, face), f32),
            pltpu.VMEM((LEVELS, 2, right, face), f32),
            pltpu.VMEM((2, nco, face), f32),
            pltpu.VMEM((2, nco, face), f32),
            pltpu.VMEM((2, face, face), bf16),
            pltpu.VMEM((2, face, face), bf16),
            pltpu.VMEM((devices, rows, nco), f32),
            pltpu.VMEM((LEVELS, devices, right // pack, lanes), f32),
            pltpu.VMEM((members, chunk, wide), f32),
            pltpu.VMEM((members, chunk, wide), f32),
            pltpu.VMEM((planes, chunk, wide), f32),
            pltpu.VMEM((members, chunk, wide), f32),
            pltpu.VMEM((members, right, wide), f32),
            pltpu.VMEM((planes, right, wide), f32),
            pltpu.VMEM((wide, half), bf16),
            pltpu.VMEM((wide, half), bf16),
            pltpu.VMEM((lanes, half), bf16),
            pltpu.VMEM((lanes, half), bf16),
            pltpu.VMEM((lanes, half), bf16),
            pltpu.VMEM((lanes, half), bf16),
            dma((6,)),
            dma((BLOCKS + 1,)),
            dma((LEVELS, 2)),
            dma((LEVELS, 2)),
            dma((LEVELS, 2)),
            dma((LEVELS, 2)),
            dma((LEVELS, 2)),
            dma((LEVELS, 2)),
            dma((2,)),
            dma((2,)),
            dma((4,)),
            dma((4,)),
            dma,
            dma,
            dma((LEVELS,)),
            dma((LEVELS,)),
            dma((3,)),
            dma((3,)),
            dma,
            dma,
            dma,
            dma,
        ],
        compiler_params=pltpu.CompilerParams(
            collective_id=0, has_side_effects=True, vmem_limit_bytes=60 * 1024 * 1024
        ),
    )(bounds, residual, local_inverse, corner_basis, corner_map, coarse_inverse)


def solution(mesh):
    in_specs = (
        P(None, "sub", "grp", None),
        P(),
        P("sub", "grp", None, None),
        P("sub", "grp", None, None),
        P("sub", "grp", None),
        P(("sub", "grp"), None),
    )
    out_specs = (P(None, None, "sub", "grp", None), P())
    run = functools.partial(body, mesh.shape["sub"], mesh.shape["grp"])
    return jax.shard_map(run, mesh=mesh, in_specs=in_specs, out_specs=out_specs, check_vma=False)
```

```python
import functools

import jax
import jax.numpy as jnp
from jax import lax
from jax.experimental import pallas as pl
from jax.experimental.pallas import tpu as pltpu
from jax.sharding import PartitionSpec as P

S_STEP = 2
BLOCKS = 2 * S_STEP + 1
LEVELS = 2 * S_STEP
LOGICAL = pl.DeviceIdType.LOGICAL
HIGHEST = lax.Precision.HIGHEST


def exact(a, b):
    return jnp.dot(a, b, precision=HIGHEST, preferred_element_type=jnp.float32)


def across_rows(a, b, precision=None):
    return lax.dot_general(
        a, b, (((1,), (1,)), ((), ())), precision=precision, preferred_element_type=jnp.float32
    )


def dot(a, b):
    return jnp.dot(a, b, preferred_element_type=jnp.float32)


def kernel(
    nsub, ngrp, inner, pack,
    bounds_hbm, res_hbm, inv_hbm, corner_hbm, map_hbm, coarse_hbm,
    basis_hbm, gram_hbm,
    basis_ref, gram_ref, bounds, res, inv, corner, ids_ref,
    up_out, up_in, diag_in, low_out, low_in, term_out, term_in, edge, cross,
    rows_c, direct, part_out, part_near, part_far, part_all, near, far,
    high, rest, load_high, load_rest, lift_high, lift_rest,
    load_sem, store_sem, up_send, up_recv, diag_send, diag_recv, low_send, low_recv,
    term_send, term_recv, edge_send, edge_recv, rows_send, rows_recv, direct_send, direct_recv,
    part_send, part_recv, near_send, near_recv, far_send, far_recv,
):
    right, half = up_out.shape[2], high.shape[1]
    face = half // 2
    order = BLOCKS * right
    nco = rows_c.shape[2]
    planes = nsub // inner
    members = inner * ngrp
    devices = nsub * ngrp
    packed_rows = right // pack
    chunk = part_out.shape[1]
    sub = lax.axis_index("sub")
    grp = lax.axis_index("grp")
    me = sub * ngrp + grp
    plane = lax.div(sub, inner)
    within = lax.rem(sub, inner)
    member = within * ngrp + grp
    sub_up, sub_down = lax.rem(sub + 1, nsub), lax.rem(sub + nsub - 1, nsub)
    grp_up, grp_down = lax.rem(grp + 1, ngrp), lax.rem(grp + ngrp - 1, ngrp)
    next_sub, prev_sub = sub_up * ngrp + grp, sub_down * ngrp + grp
    next_grp, prev_grp = sub * ngrp + grp_up, sub * ngrp + grp_down
    diagonal_peers = (sub_up * ngrp + grp_down, sub_down * ngrp + grp_up)

    def to_all(action):
        def step(offset, carry):
            other = me + offset
            action(jnp.where(other >= devices, other - devices, other))
            return carry

        lax.fori_loop(1, devices, step, 0, unroll=devices <= 64)

    near_others = [lax.rem(member + o, members) for o in range(1, members)]
    near_peers = [plane * members + o for o in near_others]
    far_peers = [lax.rem(plane + o, planes) * members + member for o in range(1, planes)]

    barrier = pltpu.get_barrier_semaphore()
    loads = [
        pltpu.make_async_copy(src, dst, load_sem.at[i])
        for i, (src, dst) in enumerate((
            (corner_hbm, corner),
            (map_hbm, ids_ref),
            (res_hbm, res),
            (coarse_hbm, rows_c.at[me]),
            (bounds_hbm, bounds),
            (inv_hbm.at[0, 0], inv),
        ))
    ]
    for copy in loads:
        copy.start()
    to_all(lambda peer: pl.semaphore_signal(barrier, inc=1, device_id=peer, device_id_type=LOGICAL))

    def send(src, dst, send_sem, recv_sem, peer):
        copy = pltpu.make_async_remote_copy(
            src_ref=src, dst_ref=dst, send_sem=send_sem, recv_sem=recv_sem,
            device_id=peer, device_id_type=LOGICAL,
        )
        copy.start()
        return copy

    pending = []
    stores = []

    def landed(buf, count, send_sem, recv_sem, peer):
        part = buf.at[pl.ds(0, count - 1)]
        copy = pltpu.make_async_remote_copy(
            src_ref=part, dst_ref=part, send_sem=send_sem, recv_sem=recv_sem,
            device_id=peer, device_id_type=LOGICAL,
        )
        copy.wait_recv()
        pending.append(copy)

    def split(value):
        rough = value.astype(jnp.bfloat16)
        return rough, (value - rough.astype(jnp.float32)).astype(jnp.bfloat16)

    def added(buf, count):
        total = buf[0]
        for i in range(1, count):
            total = total + buf[i]
        return total

    def broadcast(buf, slot, peers, send_sem, recv_sem):
        own = buf.at[slot]
        for peer in peers:
            send(own, own, send_sem, recv_sem, peer)

    def send_blocks(place, landing, corners_of):
        copies = [
            send(
                inv.at[pl.ds(first, face), pl.ds(column, face)], landing.at[d],
                edge_send.at[place + d], edge_recv.at[place + d], peer,
            )
            for d, ((first, column), peer) in enumerate(zip(corners_of, (prev_sub, prev_grp)))
        ]
        pending.extend(copies)
        return copies

    high[...] = jnp.zeros_like(high)
    rest[...] = jnp.zeros_like(rest)
    loads[0].wait()
    loads[1].wait()
    ids = ids_ref[0]
    table = (lax.broadcasted_iota(jnp.int32, (nco, ids.shape[1]), 0) == ids).astype(jnp.bfloat16)
    terms = dot(table, corner[0, 0])
    term_out[0] = terms[:, face : 2 * face]
    term_out[1] = terms[:, 3 * face :]
    for copy in loads[2:5]:
        copy.wait()
    x = res[:, 0, 0, :]
    centre = (bounds[0] + bounds[1]) / 2.0
    radius = (bounds[1] - bounds[0]) / 2.0
    scale = 1.0 / jnp.full((right, half), radius, jnp.float32)
    lane = lax.broadcasted_iota(jnp.int32, (right, pack * nco), 1)
    row = lax.broadcasted_iota(jnp.int32, (right, pack * nco), 0)
    mine = lax.div(lane, nco) == lax.div(row, packed_rows)

    def gram_part(first, second):
        both = across_rows(jnp.concatenate([first, second], axis=0), high[...])
        count = first.shape[0]
        return both[:count] + (both[count:] + across_rows(first, rest[...]))

    def coarse_part(packed):
        part = across_rows(packed, load_high[...]) + across_rows(packed, load_rest[...])
        if pack == 1:
            return part
        part = jnp.where(mine, part, 0.0)
        total = part[:packed_rows]
        for q in range(1, pack):
            total = total + part[q * packed_rows : (q + 1) * packed_rows]
        return total

    def coarse_lift(total):
        if pack > 1:
            total = jnp.where(mine, jnp.concatenate([total] * pack, axis=0), 0.0)
        total_high, total_rest = split(total)
        both = dot(jnp.concatenate([total_high, total_rest], axis=0), lift_high[...])
        return both[:right] + (both[right:] + dot(total_high, lift_rest[...]))

    def send_coarse(level, part):
        direct[level, me] = part
        own = direct.at[level, me]
        to_all(lambda peer: send(own, own, direct_send.at[level], direct_recv.at[level], peer))

    def keep(level, value):
        packed, remainder = split(value)
        basis_ref[level, :, 0, 0, :] = value
        high[pl.ds(level * right, right), :] = packed
        rest[pl.ds(level * right, right), :] = remainder
        stores.append(pltpu.make_async_copy(basis_ref.at[level], basis_hbm.at[level], store_sem.at[level]))
        stores[-1].start()
        return packed, remainder

    pl.semaphore_wait(barrier, devices - 1)
    term_copies = [
        send(term_out.at[d], term_in.at[d], term_send.at[d], term_recv.at[d], peer)
        for d, peer in enumerate((prev_sub, prev_grp))
    ]
    pending += term_copies

    previous = None
    for level in range(LEVELS):
        packed = x.astype(jnp.bfloat16)
        x_sub, x_grp = packed[:, :face], packed[:, face:]
        up_out[level, 0] = x_sub
        up_out[level, 1] = x_grp
        ups = [
            send(up_out.at[level, d], up_in.at[level, d], up_send.at[level, d], up_recv.at[level, d], peer)
            for d, peer in enumerate((next_sub, next_grp))
        ]
        diags = [
            send(up_out.at[level, d], diag_in.at[level, d], diag_send.at[level, d], diag_recv.at[level, d], peer)
            for d, peer in enumerate(diagonal_peers)
        ] if level > 0 else []
        pending += ups + diags
        if level == 0:
            own = rows_c.at[me]
            to_all(lambda peer: send(own, own, rows_send, rows_recv, peer))
            loads[5].wait()
            blocks = send_blocks(0, edge, ((face, face), (3 * face, 3 * face)))

        def own_part(first):
            columns = slice(first, first + face)
            return dot(x_sub, inv[:face, columns]) + dot(x_grp, inv[2 * face : 3 * face, columns])

        def low_part(value, first, column):
            return dot(value, inv[first : first + face, column : column + face])

        def send_lows(first, second):
            low_out[level, 0] = first
            low_out[level, 1] = second
            copies = [
                send(low_out.at[level, d], low_in.at[level, d], low_send.at[level, d], low_recv.at[level, d], peer)
                for d, peer in enumerate((prev_sub, prev_grp))
            ]
            pending.extend(copies)
            return copies

        first_low, second_low = own_part(face), own_part(3 * face)
        if level > 0:
            lows = send_lows(first_low, second_low)
            part = coarse_part(packed)
        else:
            for copy in term_copies:
                copy.wait_recv()
            weight = jnp.concatenate(
                [terms[:, :face] - term_in[0], terms[:, 2 * face : 3 * face] - term_in[1]], axis=1
            )
            weight_high, weight_rest = split(weight)
            load_high[...] = jnp.concatenate([weight_high] * pack, axis=0)
            load_rest[...] = jnp.concatenate([weight_rest] * pack, axis=0)
            part = coarse_part(packed)
        send_coarse(level, part)
        if level == 0:
            for copy in ups:
                copy.wait_recv()
            low_sub, low_grp = up_in[level, 0], up_in[level, 1]
            lows = send_lows(
                first_low - low_part(low_sub, face, face) - low_part(low_grp, 3 * face, face),
                second_low - low_part(low_sub, face, 3 * face) - low_part(low_grp, 3 * face, 3 * face),
            )
            blocks += send_blocks(2, cross, ((3 * face, face), (face, 3 * face)))
        packed, remainder = keep(level, x)
        if level == LEVELS - 1:
            count = LEVELS * right
            first_rows = gram_part(high[:count, :], rest[:count, :])
            for m in range(members):
                part_out[m] = first_rows[m * chunk : (m + 1) * chunk]
            part_near[member] = part_out[member]
            for other, peer in zip(near_others, near_peers):
                send(part_out.at[other], part_near.at[member], part_send.at[0], part_recv.at[0], peer)
        up_sub = own_part(0)
        up_grp = own_part(2 * face)
        if level > 0:
            for copy in ups:
                copy.wait_recv()
            low_sub, low_grp = up_in[level, 0], up_in[level, 1]
        up_sub = up_sub - low_part(low_sub, face, 0) - low_part(low_grp, 3 * face, 0)
        up_grp = up_grp - low_part(low_sub, face, 2 * face) - low_part(low_grp, 3 * face, 2 * face)
        if level == 0:
            landed(rows_c, devices, rows_send, rows_recv, next_grp)
            raised = exact(rows_c[...].reshape(nco, nco), weight)
            raised_high, raised_rest = split(raised)
            lift_high[...] = jnp.concatenate([raised_high] * pack, axis=0)
            lift_rest[...] = jnp.concatenate([raised_rest] * pack, axis=0)
        else:
            if level == 1:
                for copy in blocks:
                    copy.wait_recv()
            up_sub = up_sub + dot(x_sub, edge[0])
            up_grp = up_grp + dot(x_grp, edge[1])
            for copy in diags:
                copy.wait_recv()
            up_sub = up_sub + dot(diag_in[level, 1], cross[0])
            up_grp = up_grp + dot(diag_in[level, 0], cross[1])
        base = jnp.concatenate([up_sub, up_grp], axis=1) - centre * x
        for copy in lows:
            copy.wait_recv()
        base = base - jnp.concatenate([low_in[level, 0], low_in[level, 1]], axis=1)
        landed(direct.at[level], devices, direct_send.at[level], direct_recv.at[level], next_grp)
        image = base + coarse_lift(added(direct.at[level], devices))
        following = image * scale if level == 0 else 2.0 * image * scale - previous
        previous, x = x, following

    packed, remainder = keep(LEVELS, x)
    near[member] = gram_part(packed, remainder)
    broadcast(near, member, near_peers, near_send, near_recv)
    landed(part_near, members, part_send.at[0], part_recv.at[0], near_peers[0])
    part_far[plane] = added(part_near, members)
    broadcast(part_far, plane, far_peers, part_send.at[1], part_recv.at[1])
    landed(near, members, near_send, near_recv, near_peers[0])
    far[plane] = added(near, members)
    broadcast(far, plane, far_peers, far_send, far_recv)
    landed(part_far, planes, part_send.at[1], part_recv.at[1], far_peers[0])
    part_all[member] = added(part_far, planes)
    broadcast(part_all, member, near_peers, part_send.at[2], part_recv.at[2])
    landed(far, planes, far_send, far_recv, far_peers[0])
    last_rows = added(far, planes)
    landed(part_all, members, part_send.at[2], part_recv.at[2], near_peers[0])
    full = jnp.concatenate([part_all[m] for m in range(members)] + [last_rows], axis=0)[:, :order]
    row = lax.broadcasted_iota(jnp.int32, (order, order), 0)
    column = lax.broadcasted_iota(jnp.int32, (order, order), 1)
    below = jnp.where(lax.div(column, right) < lax.div(row, right), full, 0.0)
    same = jnp.where(lax.div(column, right) == lax.div(row, right), full, 0.0)
    gram_ref[...] = (below + same + below.T) * (1.0 / (half * nsub))
    stores.append(pltpu.make_async_copy(gram_ref, gram_hbm, store_sem.at[BLOCKS]))
    stores[-1].start()
    for copy in pending:
        copy.wait_send()
    for copy in stores:
        copy.wait()


def body(nsub, ngrp, residual, bounds, local_inverse, corner_basis, corner_map, coarse_inverse):
    right, half = residual.shape[0], residual.shape[3]
    face = half // 2
    width = 4 * face
    rows, nco = coarse_inverse.shape
    order = BLOCKS * right
    devices = nsub * ngrp
    inner = 1
    while nsub % (2 * inner) == 0 and 2 * inner * ngrp <= nsub // inner:
        inner *= 2
    planes, members = nsub // inner, inner * ngrp
    wide = -(-order // 128) * 128
    pack = 128 // nco if nco < 128 and 128 % nco == 0 and right % (128 // nco) == 0 else 1
    lanes = pack * nco
    chunk = LEVELS * right // members
    hbm = pl.BlockSpec(memory_space=pltpu.HBM)
    dma = pltpu.SemaphoreType.DMA
    f32, bf16 = jnp.float32, jnp.bfloat16
    return pl.pallas_call(
        functools.partial(kernel, nsub, ngrp, inner, pack),
        out_shape=(
            jax.ShapeDtypeStruct((BLOCKS, right, 1, 1, half), f32),
            jax.ShapeDtypeStruct((order, order), f32),
        ),
        in_specs=[hbm] * 6,
        out_specs=(hbm, hbm),
        scratch_shapes=[
            pltpu.VMEM((BLOCKS, right, 1, 1, half), f32),
            pltpu.VMEM((order, order), f32),
            pltpu.SMEM(bounds.shape, f32),
            pltpu.VMEM(residual.shape, f32),
            pltpu.VMEM((width, width), bf16),
            pltpu.VMEM(corner_basis.shape, bf16),
            pltpu.VMEM(corner_map.shape, corner_map.dtype),
            pltpu.VMEM((LEVELS, 2, right, face), bf16),
            pltpu.VMEM((LEVELS, 2, right, face), bf16),
            pltpu.VMEM((LEVELS, 2, right, face), bf16),
            pltpu.VMEM((LEVELS, 2, right, face), f32),
            pltpu.VMEM((LEVELS, 2, right, face), f32),
            pltpu.VMEM((2, nco, face), f32),
            pltpu.VMEM((2, nco, face), f32),
            pltpu.VMEM((2, face, face), bf16),
            pltpu.VMEM((2, face, face), bf16),
            pltpu.VMEM((devices, rows, nco), f32),
            pltpu.VMEM((LEVELS, devices, right // pack, lanes), f32),
            pltpu.VMEM((members, chunk, wide), f32),
            pltpu.VMEM((members, chunk, wide), f32),
            pltpu.VMEM((planes, chunk, wide), f32),
            pltpu.VMEM((members, chunk, wide), f32),
            pltpu.VMEM((members, right, wide), f32),
            pltpu.VMEM((planes, right, wide), f32),
            pltpu.VMEM((wide, half), bf16),
            pltpu.VMEM((wide, half), bf16),
            pltpu.VMEM((lanes, half), bf16),
            pltpu.VMEM((lanes, half), bf16),
            pltpu.VMEM((lanes, half), bf16),
            pltpu.VMEM((lanes, half), bf16),
            dma((6,)),
            dma((BLOCKS + 1,)),
            dma((LEVELS, 2)),
            dma((LEVELS, 2)),
            dma((LEVELS, 2)),
            dma((LEVELS, 2)),
            dma((LEVELS, 2)),
            dma((LEVELS, 2)),
            dma((2,)),
            dma((2,)),
            dma((4,)),
            dma((4,)),
            dma,
            dma,
            dma((LEVELS,)),
            dma((LEVELS,)),
            dma((3,)),
            dma((3,)),
            dma,
            dma,
            dma,
            dma,
        ],
        compiler_params=pltpu.CompilerParams(
            collective_id=0, has_side_effects=True, vmem_limit_bytes=60 * 1024 * 1024
        ),
    )(bounds, residual, local_inverse, corner_basis, corner_map, coarse_inverse)


def solution(mesh):
    in_specs = (
        P(None, "sub", "grp", None),
        P(),
        P("sub", "grp", None, None),
        P("sub", "grp", None, None),
        P("sub", "grp", None),
        P(("sub", "grp"), None),
    )
    out_specs = (P(None, None, "sub", "grp", None), P())
    run = functools.partial(body, mesh.shape["sub"], mesh.shape["grp"])
    return jax.shard_map(run, mesh=mesh, in_specs=in_specs, out_specs=out_specs, check_vma=False)
```
